32 devices in a mesh: dp: 8 (over y, x, core), tensor: 4 (over z).
Axes of the slice: x: 2, y: 2, z: 4, core: 2. Of those that a mesh axis runs over, the one named last changes fastest.
Arguments:
- kv_part: bfloat16 [4, 2048, 12288], P('tensor', 'dp'), may hold values from -2 to 2
- queries: bfloat16 [4096, 6144], P('dp', 'tensor'), may hold values from -6 to 6
- w_out: bfloat16 [6144, 8192], P('tensor'), may hold values from -0.078125 to 0.078125
- d_out: bfloat16 [4096, 8192], P('dp', 'tensor'), may hold values from -48 to 48
- nbr_owner: int32 [64, 2], replicated, may hold values from 0 to 7, as said below
- nbr_slot: int32 [64, 2], replicated, may hold values from 0 to 1, as said below
Outputs:
- mixed: bfloat16 [4096, 8192], P('dp', 'tensor')
- d_kv: bfloat16 [2048, 12288], P('dp', 'tensor')
The draws below stay inside these ranges and needn't reach their ends.
Inputs may be any that keep to these rules, and one draw needn't show every extreme that they name: `nbr_owner`: the two neighbours of one span have different owners. `nbr_slot`: all neighbours that the spans of one dp index r (spans r * 8 to (r + 1) * 8 - 1) take from one owner have the same slot.
All inputs are finite; a program needn't handle non-finite values.
Results may differ from the reference program's by a relative error of at most 0.025.
Values may be sent and summed in bfloat16 or wider, within the bound.
No kernel may reach another device: no remote copies, remote signals or barrier semaphores. Data moves between devices by JAX's collectives and lax.ppermute only.
A program may use at most 192 MiB of HBM per device.

```python
import jax
import jax.numpy as jnp
from jax import lax

D = 8192
HEADS = 48
HD = 128
SPAN = 64
NBR_LEN = 128
NB_DEV = 2
CH_DEV = 8
SPANS = 64
TOKENS = 4096
NBRS = 16
AW = 6144
KVW = 12288
N_DP = 8
N_TENSOR = 4


def neighbour_tables(key):
    base = jax.random.fold_in(key, 101)
    first_key, second_key, third_key, fourth_key = jax.random.split(base, 4)
    span_ids = jnp.arange(SPANS, dtype=jnp.int32)
    order = jax.random.permutation(first_key, N_DP).astype(jnp.int32)
    shifts = jax.random.randint(second_key, (SPANS,), 0, N_DP, dtype=jnp.int32)
    first = (order[span_ids % N_DP] + shifts[span_ids // N_DP]) % N_DP
    second = (first + jax.random.randint(third_key, (SPANS,), 1, N_DP, dtype=jnp.int32)) % N_DP
    owners = jnp.stack([first, second], axis=1)
    table = jax.random.randint(fourth_key, (N_DP, N_DP), 0, NB_DEV, dtype=jnp.int32)
    table = table.at[0, first[0]].set(NB_DEV - 1)
    table = table.at[0, second[0]].set(0)
    readers = span_ids // CH_DEV
    slots = table[readers[:, None], owners]
    return (owners, slots)


def draw_nbr_owner(key, part):
    return neighbour_tables(key)[0]


def draw_nbr_slot(key, part):
    return neighbour_tables(key)[1]


def draw_kv_part(key, part):
    spread = N_TENSOR ** (-0.5)
    shape = (N_TENSOR, NBRS * NBR_LEN, KVW)
    values = jnp.clip(jax.random.normal(jax.random.fold_in(key, 303), shape, jnp.float32) * spread, -2.0, 2.0)
    return values.astype(jnp.bfloat16)


def draw_queries(key, part):
    shape = (TOKENS, AW)
    values = jnp.clip(jax.random.normal(jax.random.fold_in(key, 404), shape, jnp.float32), -6.0, 6.0)
    return values.astype(jnp.bfloat16)


def block_scale(own_key, extent, cuts, least, top_value):
    gain, own = 1.0, jax.random.fold_in(own_key, 6)
    for dim, shards_of in cuts:
        draws = jnp.exp(jax.random.uniform(jax.random.fold_in(own, dim), (shards_of,), jnp.float32, least / len(cuts), top_value / len(cuts)))
        gain = gain * jnp.repeat(draws, extent[dim] // shards_of).reshape([-1 if axis == dim else 1 for axis in range(len(extent))])
    return gain


def scatter_about(rng, extent, deviation, limit, cuts=(), kind=jnp.bfloat16):
    result = deviation * jax.random.normal(rng, extent, jnp.float32)
    if cuts:
        result = result * block_scale(rng, extent, cuts, -0.22, 0.18)
    return jnp.clip(result, -limit, limit).astype(kind)


def setup_inputs(seed: int = 0) -> dict:
    seeds = jax.random.split(jax.random.key(seed), 7)
    return {
        "kv_part": draw_kv_part(jax.random.fold_in(seeds[6], 71), 0),
        "queries": draw_queries(jax.random.fold_in(seeds[6], 71), 0),
        "w_out": scatter_about(seeds[2], (AW, D), AW ** -0.5, 0.078125, ((0, 4),)),
        "d_out": scatter_about(seeds[3], (TOKENS, D), 8.0, 48.0, ((0, 8), (1, 4))),
        "nbr_owner": draw_nbr_owner(jax.random.fold_in(seeds[6], 71), 0),
        "nbr_slot": draw_nbr_slot(jax.random.fold_in(seeds[6], 71), 0),
    }


def reference(kv_part, queries, w_out, d_out, nbr_owner, nbr_slot):
    kv_sum = jnp.sum(kv_part.astype(jnp.float32), axis=0).astype(jnp.bfloat16)
    kv_blocks = kv_sum.reshape(NBRS, NBR_LEN * KVW)
    grad_attended = jnp.dot(d_out, w_out.T, preferred_element_type=jnp.float32).astype(jnp.bfloat16)
    factor = HD ** -0.5
    owner_ids = jnp.arange(N_DP, dtype=jnp.int32)
    neighbour_ids = jnp.arange(NBRS, dtype=jnp.int32)

    def per_reader(total, reader):
        owners = lax.dynamic_slice_in_dim(nbr_owner, reader * CH_DEV, CH_DEV, 0).reshape(2 * CH_DEV)
        slots = lax.dynamic_slice_in_dim(nbr_slot, reader * CH_DEV, CH_DEV, 0).reshape(2 * CH_DEV)
        picked = jnp.take(kv_blocks, owners * NB_DEV + slots, axis=0)
        layout = picked.reshape(CH_DEV, 2 * NBR_LEN, HEADS, 2, HD).astype(jnp.float32)
        keys = layout[:, :, :, 0]
        values = layout[:, :, :, 1]
        query_rows = lax.dynamic_slice_in_dim(queries, reader * CH_DEV * SPAN, CH_DEV * SPAN, 0)
        query_view = query_rows.astype(jnp.float32).reshape(CH_DEV, SPAN, HEADS, HD)
        scores = jnp.einsum("cqhd,ckhd->chqk", query_view, keys, precision=lax.Precision.HIGHEST) * factor
        top = jnp.max(scores, axis=-1, keepdims=True)
        expo = jnp.exp(scores - top)
        probs = expo / jnp.sum(expo, axis=-1, keepdims=True)
        probs_low = probs.astype(jnp.bfloat16).astype(jnp.float32)
        attended = jnp.einsum("chqk,ckhd->cqhd", probs_low, values, precision=lax.Precision.HIGHEST).astype(jnp.bfloat16)
        grad_rows = lax.dynamic_slice_in_dim(grad_attended, reader * CH_DEV * SPAN, CH_DEV * SPAN, 0)
        grad_view = grad_rows.astype(jnp.float32).reshape(CH_DEV, SPAN, HEADS, HD)
        grad_values = jnp.einsum("chqk,cqhd->ckhd", probs_low, grad_view, precision=lax.Precision.HIGHEST)
        grad_probs = jnp.einsum("cqhd,ckhd->chqk", grad_view, values, precision=lax.Precision.HIGHEST)
        grad_scores = probs * (grad_probs - jnp.sum(probs * grad_probs, axis=-1, keepdims=True))
        grad_scores = grad_scores.astype(jnp.bfloat16).astype(jnp.float32)
        grad_keys = jnp.einsum("chqk,cqhd->ckhd", grad_scores, query_view, precision=lax.Precision.HIGHEST) * factor
        grad_blocks = jnp.stack([grad_keys, grad_values], axis=3).reshape(2 * CH_DEV, NBR_LEN * KVW)
        read_table = (owners[:, None] == owner_ids[None, :]).astype(jnp.float32)
        per_owner = jnp.dot(read_table.T, grad_blocks, precision=lax.Precision.HIGHEST).astype(jnp.bfloat16)
        per_owner = lax.optimization_barrier(per_owner).astype(jnp.float32)
        hits = owners[:, None] == owner_ids[None, :]
        reads_from = jnp.any(hits, axis=0)
        slot_from = jnp.max(jnp.where(hits, slots[:, None], 0), axis=0)
        target = owner_ids * NB_DEV + slot_from
        routing = ((target[:, None] == neighbour_ids[None, :]) & reads_from[:, None]).astype(jnp.float32)
        total = total + jnp.dot(routing.T, per_owner, precision=lax.Precision.HIGHEST)
        return total, attended.reshape(CH_DEV * SPAN, AW)

    total, attended_all = lax.scan(per_reader, jnp.zeros((NBRS, NBR_LEN * KVW), jnp.float32), jnp.arange(N_DP, dtype=jnp.int32))
    attended_all = attended_all.reshape(TOKENS, AW)
    group_width = AW // N_TENSOR

    def add_group(group, running):
        columns = lax.dynamic_slice_in_dim(attended_all, group * group_width, group_width, 1)
        rows = lax.dynamic_slice_in_dim(w_out, group * group_width, group_width, 0)
        partial_value = jnp.dot(columns, rows, preferred_element_type=jnp.float32).astype(jnp.bfloat16)
        partial_value = lax.optimization_barrier(partial_value)
        return running + partial_value.astype(jnp.float32)

    mixed = lax.fori_loop(0, N_TENSOR, add_group, jnp.zeros((TOKENS, D), jnp.float32)).astype(jnp.bfloat16)
    d_kv = total.astype(jnp.bfloat16).reshape(NBRS * NBR_LEN, KVW)
    return mixed, d_kv
```

```python
import functools

import jax
import jax.numpy as jnp
from jax import lax
from jax.experimental import pallas as pl
from jax.experimental.pallas import tpu as pltpu
from jax.sharding import PartitionSpec as P

HD = 128
SPAN = 64
NBR_LEN = 128
NB_DEV = 2
NT = (((1,), (1,)), ((), ()))
BIG_VMEM = 56 * 1024 * 1024


def pair_of(first, second, column):
    return jnp.concatenate(
        [first[0, :, column : column + HD], second[0, :, column : column + HD]], axis=0
    )


def attend_kernel(heads, ids_ref, q_ref, first_ref, second_ref, out_ref):
    del ids_ref
    for head in range(heads):
        at = head * HD
        keys = pair_of(first_ref, second_ref, 2 * at)
        values = pair_of(first_ref, second_ref, 2 * at + HD)
        scores = lax.dot_general(
            q_ref[:, at : at + HD], keys, NT, preferred_element_type=jnp.float32
        ) * (HD**-0.5)
        expo = jnp.exp(scores - jnp.max(scores, axis=1, keepdims=True))
        probs = expo / jnp.sum(expo, axis=1, keepdims=True)
        out = jnp.dot(probs.astype(jnp.bfloat16), values, preferred_element_type=jnp.float32)
        out_ref[:, at : at + HD] = out.astype(jnp.bfloat16)


def attend(ids, queries, blocks):
    tokens, width = queries.shape
    spans = tokens // SPAN
    share = blocks.shape[2]
    return pl.pallas_call(
        functools.partial(attend_kernel, width // HD),
        grid_spec=pltpu.PrefetchScalarGridSpec(
            num_scalar_prefetch=1,
            grid=(spans,),
            in_specs=[
                pl.BlockSpec((SPAN, width), lambda c, ids: (c, 0)),
                pl.BlockSpec((1, NBR_LEN, share), lambda c, ids: (ids[2 * c], 0, 0)),
                pl.BlockSpec((1, NBR_LEN, share), lambda c, ids: (ids[2 * c + 1], 0, 0)),
            ],
            out_specs=pl.BlockSpec((SPAN, width), lambda c, ids: (c, 0)),
        ),
        out_shape=jax.ShapeDtypeStruct((tokens, width), jnp.bfloat16),
        compiler_params=pltpu.CompilerParams(vmem_limit_bytes=BIG_VMEM),
        cost_estimate=pl.CostEstimate(
            flops=8 * tokens * NBR_LEN * width,
            bytes_accessed=4 * tokens * width + 4 * spans * NBR_LEN * share,
            transcendentals=2 * tokens * NBR_LEN * width // HD,
        ),
        name="attend",
    )(ids, queries, blocks, blocks)


def attend_grad_kernel(
    heads, ids_ref, own_ref, q_ref, g_ref, first_ref, second_ref, out_ref, total_ref
):
    del ids_ref
    span = pl.program_id(1)

    @pl.when(span == 0)
    def _():
        total_ref[...] = jnp.zeros_like(total_ref)

    owner_a = own_ref[2 * span]
    owner_b = own_ref[2 * span + 1]
    factor = HD**-0.5
    for head in range(heads):
        at = head * HD
        query = q_ref[:, at : at + HD]
        grad = g_ref[:, at : at + HD]
        keys = pair_of(first_ref, second_ref, 2 * at)
        values = pair_of(first_ref, second_ref, 2 * at + HD)
        scores = lax.dot_general(keys, query, NT, preferred_element_type=jnp.float32) * factor
        expo = jnp.exp(scores - jnp.max(scores, axis=0, keepdims=True))
        probs = expo / jnp.sum(expo, axis=0, keepdims=True)
        grad_probs = lax.dot_general(values, grad, NT, preferred_element_type=jnp.float32)
        inner = jnp.sum(probs * grad_probs, axis=0, keepdims=True)
        grad_scores = (probs * (grad_probs - inner)).astype(jnp.bfloat16)
        grad_keys = jnp.dot(grad_scores, query, preferred_element_type=jnp.float32) * factor
        grad_values = jnp.dot(
            probs.astype(jnp.bfloat16), grad, preferred_element_type=jnp.float32
        )
        key_at = slice(2 * at, 2 * at + HD)
        value_at = slice(2 * at + HD, 2 * at + 2 * HD)
        total_ref[owner_a, :, key_at] += grad_keys[:NBR_LEN]
        total_ref[owner_b, :, key_at] += grad_keys[NBR_LEN:]
        total_ref[owner_a, :, value_at] += grad_values[:NBR_LEN]
        total_ref[owner_b, :, value_at] += grad_values[NBR_LEN:]

    @pl.when(span == pl.num_programs(1) - 1)
    def _():
        out_ref[...] = total_ref[...].astype(jnp.bfloat16)


def attend_grad(ids, owners, owner_count, queries, grads, blocks, groups):
    tokens, width = queries.shape
    spans = tokens // SPAN
    share = blocks.shape[2]
    part, share_part = width // groups, share // groups
    return pl.pallas_call(
        functools.partial(attend_grad_kernel, part // HD),
        grid_spec=pltpu.PrefetchScalarGridSpec(
            num_scalar_prefetch=2,
            grid=(groups, spans),
            in_specs=[
                pl.BlockSpec((SPAN, part), lambda g, c, ids, own: (c, g)),
                pl.BlockSpec((SPAN, part), lambda g, c, ids, own: (c, g)),
                pl.BlockSpec(
                    (1, NBR_LEN, share_part), lambda g, c, ids, own: (ids[2 * c], 0, g)
                ),
                pl.BlockSpec(
                    (1, NBR_LEN, share_part), lambda g, c, ids, own: (ids[2 * c + 1], 0, g)
                ),
            ],
            out_specs=pl.BlockSpec(
                (owner_count, NBR_LEN, share_part), lambda g, c, ids, own: (0, 0, g)
            ),
            scratch_shapes=[pltpu.VMEM((owner_count, NBR_LEN, share_part), jnp.float32)],
        ),
        out_shape=jax.ShapeDtypeStruct((owner_count, NBR_LEN, share), jnp.bfloat16),
        compiler_params=pltpu.CompilerParams(vmem_limit_bytes=BIG_VMEM),
        cost_estimate=pl.CostEstimate(
            flops=20 * tokens * NBR_LEN * width,
            bytes_accessed=4 * tokens * width
            + 4 * spans * NBR_LEN * share
            + 2 * owner_count * NBR_LEN * share,
            transcendentals=2 * tokens * NBR_LEN * width // HD,
        ),
        name="attend_grad",
    )(ids, owners, queries, grads, blocks, blocks)


def line_reduce_scatter(term, me, count, chunks):
    right = [None] * chunks
    left = [None] * chunks
    for step in range(1, count):
        rightward = [(i, i + 1) for i in range(step)]
        leftward = [(i, i - 1) for i in range(count - step, count)]
        to_right = me + count - step
        to_left = me - count + step
        for c in range(chunks):
            if 2 * step <= count:
                total = term(c, jnp.where(me < step, to_right, jnp.maximum(to_left, 0)))
                if step > 1:
                    total = total + right[c].astype(jnp.float32) + left[c].astype(jnp.float32)
                total = total.astype(jnp.bfloat16)
                right_total, left_total = total, total
            else:
                right_total = term(c, jnp.minimum(to_right, count - 1))
                right_total = (right_total + right[c].astype(jnp.float32)).astype(jnp.bfloat16)
                left_total = term(c, jnp.maximum(to_left, 0))
                left_total = (left_total + left[c].astype(jnp.float32)).astype(jnp.bfloat16)
            right[c] = lax.ppermute(right_total, "tensor", rightward)
            left[c] = lax.ppermute(left_total, "tensor", leftward)
    return [
        term(c, me) + right[c].astype(jnp.float32) + left[c].astype(jnp.float32)
        for c in range(chunks)
    ]


def line_all_gather(block, count):
    right, left = [block], [block]
    for step in range(1, count):
        rightward = [(i, i + 1) for i in range(step - 1, count - 1)]
        leftward = [(i, i - 1) for i in range(1, count - step + 1)]
        right.append(lax.ppermute(right[-1], "tensor", rightward))
        left.append(lax.ppermute(left[-1], "tensor", leftward))
    return [block] + [left[s] + right[count - s] for s in range(1, count)]


def local(kv_part, queries, w_out, d_out, nbr_owner, nbr_slot):
    dp_count = lax.axis_size("dp")
    tensor_count = lax.axis_size("tensor")
    reader = lax.axis_index("dp")
    me = lax.axis_index("tensor")
    tokens, head_width = queries.shape
    share_width = 2 * head_width
    span_count = tokens // SPAN
    read_count = 2 * span_count
    out_width = d_out.shape[1]

    owner_ids = jnp.arange(dp_count, dtype=jnp.int32)
    per_reader = (nbr_owner[:, :, None] == owner_ids[None, None, :]).reshape(
        dp_count, read_count, dp_count
    )
    slot_from = jnp.max(
        jnp.where(per_reader, nbr_slot.reshape(dp_count, read_count, 1), 0), axis=1
    )
    serving_slot = lax.dynamic_index_in_dim(slot_from, reader, 1, False)
    owners = lax.dynamic_slice_in_dim(nbr_owner, reader * span_count, span_count, 0).reshape(
        read_count
    )
    slots = lax.dynamic_slice_in_dim(nbr_slot, reader * span_count, span_count, 0).reshape(
        read_count
    )
    ids = owners * NB_DEV + slots

    def kv_term(chunk, shard):
        rows = kv_part[0, chunk * NBR_LEN : (chunk + 1) * NBR_LEN]
        return lax.dynamic_slice_in_dim(rows, shard * share_width, share_width, 1).astype(
            jnp.float32
        )

    summed = line_reduce_scatter(kv_term, me, tensor_count, NB_DEV)
    share = jnp.stack([part.astype(jnp.bfloat16) for part in summed])
    blocks = lax.all_gather(share, "dp", axis=0, tiled=True)

    attended = attend(ids, queries, blocks)
    row_chunks = 2
    rows = tokens // row_chunks

    def mixed_term(chunk, shard):
        weights = lax.dynamic_slice_in_dim(w_out, shard * out_width, out_width, 1)
        return jnp.dot(
            attended[chunk * rows : (chunk + 1) * rows],
            weights,
            preferred_element_type=jnp.float32,
        )

    mixed = line_reduce_scatter(mixed_term, me, tensor_count, row_chunks)
    mixed = jnp.concatenate([part.astype(jnp.bfloat16) for part in mixed])

    grads = []
    for chunk in range(row_chunks):
        pieces = line_all_gather(d_out[chunk * rows : (chunk + 1) * rows], tensor_count)
        total = jnp.zeros((rows, head_width), jnp.float32)
        for s in [0] + sorted(range(1, tensor_count), key=lambda s: abs(2 * s - tensor_count)):
            weights = lax.dynamic_slice_in_dim(
                w_out, lax.rem(me + s, tensor_count) * out_width, out_width, 1
            )
            total = total + lax.dot_general(
                pieces[s], weights, NT, preferred_element_type=jnp.float32
            )
        grads.append(total.astype(jnp.bfloat16))
    grad_attended = jnp.concatenate(grads)
    per_owner = attend_grad(ids, owners, dp_count, queries, grad_attended, blocks, 2)
    returned = lax.all_to_all(per_owner, "dp", split_axis=0, concat_axis=0, tiled=True)
    picked = [
        jnp.sum(
            jnp.where((serving_slot == slot)[:, None, None], returned.astype(jnp.float32), 0.0),
            axis=0,
        )
        for slot in range(NB_DEV)
    ]
    d_kv = jnp.concatenate(picked).astype(jnp.bfloat16)
    return (mixed, d_kv)


def solution(mesh):
    placed = (
        P("tensor", "dp", None),
        P("dp", "tensor"),
        P("tensor", None),
        P("dp", "tensor"),
        P(),
        P(),
    )
    return jax.shard_map(
        local,
        mesh=mesh,
        in_specs=placed,
        out_specs=(P("dp", "tensor"), P("dp", "tensor")),
        check_vma=False,
    )
```

```python
import functools

import jax
import jax.numpy as jnp
from jax import lax
from jax.experimental import pallas as pl
from jax.experimental.pallas import tpu as pltpu
from jax.sharding import PartitionSpec as P

HD = 128
SPAN = 64
NBR_LEN = 128
NB_DEV = 2
NT = (((1,), (1,)), ((), ()))
MIB = 1024 * 1024
SMALL = pl.CostEstimate(flops=1, bytes_accessed=1, transcendentals=0)


def pair_of(first, second, column):
    return jnp.concatenate(
        [first[0, :, column : column + HD], second[0, :, column : column + HD]], axis=0
    )


def two_heads_of(first, second, head, offset):
    left, right = 2 * head * HD + offset, 2 * (head + 1) * HD + offset
    rows = [
        jnp.concatenate([ref[0, :, left : left + HD], ref[0, :, right : right + HD]], axis=1)
        for ref in (first, second)
    ]
    return jnp.concatenate(rows, axis=0)


def block_diagonal(ref, rows, head):
    left = ref[rows, head * HD : (head + 1) * HD]
    right = ref[rows, (head + 1) * HD : (head + 2) * HD]
    blank = jnp.zeros_like(left)
    return jnp.concatenate(
        [jnp.concatenate([left, blank], axis=1), jnp.concatenate([blank, right], axis=1)], axis=0
    )


def attend_kernel(heads, ids_ref, q_ref, *refs):
    del ids_ref
    out_ref = refs[-1]
    every = [(c, h) for c in range(len(refs) // 2) for h in range(heads)]
    rows = [slice(c * SPAN, (c + 1) * SPAN) for c, _ in every]
    scores = [
        lax.dot_general(
            q_ref[r, h * HD : (h + 1) * HD],
            pair_of(refs[2 * c], refs[2 * c + 1], 2 * h * HD),
            NT,
            preferred_element_type=jnp.float32,
        )
        for r, (c, h) in zip(rows, every)
    ]
    highest = [jnp.max(s, axis=1, keepdims=True) for s in scores]
    expo = [jnp.exp((s - m) * (HD**-0.5)) for s, m in zip(scores, highest)]
    inverse = [1.0 / jnp.sum(e, axis=1, keepdims=True) for e in expo]
    probs = [(e * r).astype(jnp.bfloat16) for e, r in zip(expo, inverse)]
    for p, r, (c, h) in zip(probs, rows, every):
        values = pair_of(refs[2 * c], refs[2 * c + 1], 2 * h * HD + HD)
        out = jnp.dot(p, values, preferred_element_type=jnp.float32)
        out_ref[r, h * HD : (h + 1) * HD] = out.astype(jnp.bfloat16)


def neighbour_specs(group, share):
    def spec(place):
        return pl.BlockSpec(
            (1, NBR_LEN, share), lambda c, ids, *_: (ids[2 * group * c + place], 0, 0)
        )

    return [spec(place) for place in range(2 * group)]


def attend(ids, queries, blocks, part):
    tokens = queries.shape[0]
    spans = tokens // SPAN
    share = blocks.shape[2]
    width = share // 2
    group = 2 if spans % 2 == 0 else 1
    return pl.pallas_call(
        functools.partial(attend_kernel, width // HD),
        grid_spec=pltpu.PrefetchScalarGridSpec(
            num_scalar_prefetch=1,
            grid=(spans // group,),
            in_specs=[pl.BlockSpec((group * SPAN, width), lambda c, ids: (c, part))]
            + neighbour_specs(group, share),
            out_specs=pl.BlockSpec((group * SPAN, width), lambda c, ids: (c, 0)),
        ),
        out_shape=jax.ShapeDtypeStruct((tokens, width), jnp.bfloat16),
        compiler_params=pltpu.CompilerParams(vmem_limit_bytes=42 * MIB),
        cost_estimate=SMALL,
        name="attend",
    )(ids, queries, *([blocks] * (2 * group)))


def attend_grad_kernel(group, parts, ids_ref, own_ref, q_ref, g_ref, *refs):
    del ids_ref
    out_ref, total_ref = refs[-2:]
    step = pl.program_id(0)

    @pl.when(step == 0)
    def _():
        total_ref[...] = jnp.zeros_like(total_ref)

    factor = HD**-0.5
    heads = q_ref.shape[1] // HD
    part_heads = heads // parts
    for c in range(group):
        tokens = slice(c * SPAN, (c + 1) * SPAN)
        places = (
            (own_ref[2 * (group * step + c)], slice(0, NBR_LEN)),
            (own_ref[2 * (group * step + c) + 1], slice(NBR_LEN, 2 * NBR_LEN)),
        )
        for part in range(parts):
            first_ref, second_ref = refs[2 * (group * part + c) : 2 * (group * part + c) + 2]
            pairs = range(0, part_heads, 2)
            query = [block_diagonal(q_ref, tokens, part * part_heads + h) for h in pairs]
            grad = [block_diagonal(g_ref, tokens, part * part_heads + h) for h in pairs]
            scores = [
                lax.dot_general(
                    two_heads_of(first_ref, second_ref, h, 0),
                    x,
                    NT,
                    preferred_element_type=jnp.float32,
                )
                for h, x in zip(pairs, query)
            ]
            grad_probs = [
                lax.dot_general(
                    two_heads_of(first_ref, second_ref, h, HD),
                    x,
                    NT,
                    preferred_element_type=jnp.float32,
                )
                for h, x in zip(pairs, grad)
            ]
            highest = [jnp.max(s, axis=0, keepdims=True) for s in scores]
            expo = [jnp.exp((s - m) * factor) for s, m in zip(scores, highest)]
            inverse = [1.0 / jnp.sum(e, axis=0, keepdims=True) for e in expo]
            probs = [e * r for e, r in zip(expo, inverse)]
            inner = [jnp.sum(p * d, axis=0, keepdims=True) for p, d in zip(probs, grad_probs)]
            grad_scores = [
                (p * (d - i)).astype(jnp.bfloat16) for p, d, i in zip(probs, grad_probs, inner)
            ]
            grad_keys = [
                jnp.dot(d, x, preferred_element_type=jnp.float32)
                for d, x in zip(grad_scores, query)
            ]
            grad_values = [
                jnp.dot(p.astype(jnp.bfloat16), x, preferred_element_type=jnp.float32)
                for p, x in zip(probs, grad)
            ]
            for h, keys, values in zip(pairs, grad_keys, grad_values):
                for i in range(2):
                    at = 2 * (part * part_heads + h + i) * HD
                    lanes = slice(i * HD, (i + 1) * HD)
                    for owner, rows in places:
                        total_ref[owner, :, at : at + HD] += keys[rows, lanes]
                        total_ref[owner, :, at + HD : at + 2 * HD] += values[rows, lanes]

    @pl.when(step == pl.num_programs(0) - 1)
    def _():
        for h in range(heads):
            at = 2 * h * HD
            out_ref[:, :, at : at + HD] = (total_ref[:, :, at : at + HD] * factor).astype(
                jnp.bfloat16
            )
            out_ref[:, :, at + HD : at + 2 * HD] = total_ref[
                :, :, at + HD : at + 2 * HD
            ].astype(jnp.bfloat16)


def attend_grad(ids, owners, owner_count, queries, grads, blocks):
    tokens, width = queries.shape
    spans = tokens // SPAN
    parts = len(blocks)
    part_share = blocks[0].shape[2]
    share = parts * part_share
    group = 2 if spans % 2 == 0 else 1
    return pl.pallas_call(
        functools.partial(attend_grad_kernel, group, parts),
        grid_spec=pltpu.PrefetchScalarGridSpec(
            num_scalar_prefetch=2,
            grid=(spans // group,),
            in_specs=[pl.BlockSpec((group * SPAN, width), lambda c, ids, own: (c, 0))] * 2
            + neighbour_specs(group, part_share) * parts,
            out_specs=pl.BlockSpec(
                (owner_count, NBR_LEN, share), lambda c, ids, own: (0, 0, 0)
            ),
            scratch_shapes=[pltpu.VMEM((owner_count, NBR_LEN, share), jnp.float32)],
        ),
        out_shape=jax.ShapeDtypeStruct((owner_count, NBR_LEN, share), jnp.bfloat16),
        compiler_params=pltpu.CompilerParams(vmem_limit_bytes=50 * MIB),
        cost_estimate=SMALL,
        name="attend_grad",
    )(ids, owners, queries, grads, *[b for b in blocks for _ in range(2 * group)])


def tile_of(width):
    return next(tile for tile in (512, 384, 256, HD) if width % tile == 0)


def project_kernel(parts, received, shard_ref, *refs):
    del shard_ref
    inputs, weights = refs[:parts], refs[parts : 2 * parts]
    total = jnp.dot(inputs[0][...], weights[0][...], preferred_element_type=jnp.float32)
    for x, w in zip(inputs[1:], weights[1:]):
        total = total + jnp.dot(x[...], w[...], preferred_element_type=jnp.float32)
    for r in refs[2 * parts : 2 * parts + received]:
        total = total + r[...].astype(jnp.float32)
    refs[-1][...] = total.astype(jnp.bfloat16)


def project(shard, inputs, w_out, width, received):
    parts = len(inputs)
    tokens, depth = inputs[0].shape
    tile = tile_of(width)
    steps = width // tile

    def weights_of(part):
        return pl.BlockSpec((depth, tile), lambda j, s: (part, s[0] * steps + j))

    return pl.pallas_call(
        functools.partial(project_kernel, parts, len(received)),
        grid_spec=pltpu.PrefetchScalarGridSpec(
            num_scalar_prefetch=1,
            grid=(steps,),
            in_specs=[pl.BlockSpec((tokens, depth), lambda j, s: (0, 0))] * parts
            + [weights_of(part) for part in range(parts)]
            + [pl.BlockSpec((tokens, tile), lambda j, s: (0, j))] * len(received),
            out_specs=pl.BlockSpec((tokens, tile), lambda j, s: (0, j)),
        ),
        out_shape=jax.ShapeDtypeStruct((tokens, width), jnp.bfloat16),
        compiler_params=pltpu.CompilerParams(vmem_limit_bytes=42 * MIB),
        cost_estimate=SMALL,
        name="project",
    )(shard.reshape(1), *inputs, *([w_out] * parts), *received)


def back_project_kernel(counts, carried, shards_ref, *refs):
    del shards_ref
    weights, out_ref = refs[: len(counts)], refs[-1]
    total = refs[-2][...] if carried else None
    at = len(counts)
    for count, weight in zip(counts, weights):
        block = refs[at][...]
        for other in refs[at + 1 : at + count]:
            block = block + other[...]
        at += count
        term = lax.dot_general(block, weight[...], NT, preferred_element_type=jnp.float32)
        total = term if total is None else total + term
    out_ref[...] = total.astype(out_ref.dtype)


def back_project(groups, w_out, carry, out_type):
    tokens, depth = groups[0][1][0].shape
    head_width = w_out.shape[0]
    tile = tile_of(head_width)
    blocks = [block for _, sources in groups for block in sources]
    extra = [] if carry is None else [carry]

    def weights_of(group):
        return pl.BlockSpec((tile, depth), lambda j, s: (j, s[group]))

    return pl.pallas_call(
        functools.partial(
            back_project_kernel, [len(sources) for _, sources in groups], carry is not None
        ),
        grid_spec=pltpu.PrefetchScalarGridSpec(
            num_scalar_prefetch=1,
            grid=(head_width // tile,),
            in_specs=[weights_of(group) for group in range(len(groups))]
            + [pl.BlockSpec((tokens, depth), lambda j, s: (0, 0), pipeline_mode=pl.Buffered(1))]
            * len(blocks)
            + [pl.BlockSpec((tokens, tile), lambda j, s: (0, j))] * len(extra),
            out_specs=pl.BlockSpec((tokens, tile), lambda j, s: (0, j)),
        ),
        out_shape=jax.ShapeDtypeStruct((tokens, head_width), out_type),
        compiler_params=pltpu.CompilerParams(vmem_limit_bytes=48 * MIB),
        cost_estimate=SMALL,
        name="back_project",
    )(jnp.stack([shard for shard, _ in groups]), *([w_out] * len(groups)), *blocks, *extra)


def after(x, *others):
    return lax.optimization_barrier((x, *others))[0]


FAR, NEAR, BESIDE = (3, 3, 0, 0), (2, 2, 1, 1), (1, 0, 3, 2)
INWARDS = [(0, 1), (3, 2)]
OUTWARDS = [(1, 0), (2, 3)]
SWAP = [(0, 1), (1, 0), (2, 3), (3, 2)]
ACROSS = [(1, 2), (2, 1)]
TWO_ON = [(1, 3), (2, 0)]
TWO_IN = [(3, 1), (0, 2)]


def send(x, hops):
    return lax.ppermute(x, "tensor", hops)


def entry(table, me):
    return jnp.take(jnp.array(table, jnp.int32), me)


class LineSum:
    def __init__(self, term, me):
        self.term, self.me = term, me
        self.far = term(entry(FAR, me), [])
        self.far_in = send(self.far, INWARDS)
        self.near = term(after(entry(NEAR, me), self.far), [])
        self.near_in = send(self.near, INWARDS)
        self.beside = term(after(entry(BESIDE, me), self.near), [])
        self.beside_in = send(self.beside, SWAP)

    def add_far(self, *others):
        self.far_sum = self.far + after(self.far_in, *others)
        self.far_in = send(self.far_sum, TWO_ON)

    def add_near(self, *others):
        self.near_sum = self.near + after(self.near_in, *others)
        self.near_in = send(self.near_sum, ACROSS)

    def finish(self):
        return self.term(self.me, [self.beside_in, self.far_in, self.near_in])


def settle_kernel(slot_ref, returned_ref, out_ref):
    totals = [jnp.zeros(returned_ref.shape[1:], jnp.float32) for _ in range(NB_DEV)]
    for r in range(returned_ref.shape[0]):
        block = returned_ref[r].astype(jnp.float32)
        for slot in range(NB_DEV):
            totals[slot] = totals[slot] + jnp.where(slot_ref[r] == slot, block, 0.0)
    for slot in range(NB_DEV):
        out_ref[slot * NBR_LEN : (slot + 1) * NBR_LEN] = totals[slot].astype(jnp.bfloat16)


def settle(slots, returned):
    readers, _, width = returned.shape
    tile = next(tile for tile in (1024, 768, 512, 256, HD) if width % tile == 0)
    return pl.pallas_call(
        settle_kernel,
        grid_spec=pltpu.PrefetchScalarGridSpec(
            num_scalar_prefetch=1,
            grid=(width // tile,),
            in_specs=[pl.BlockSpec((readers, NBR_LEN, tile), lambda j, s: (0, 0, j))],
            out_specs=pl.BlockSpec((NB_DEV * NBR_LEN, tile), lambda j, s: (0, j)),
        ),
        out_shape=jax.ShapeDtypeStruct((NB_DEV * NBR_LEN, width), jnp.bfloat16),
        compiler_params=pltpu.CompilerParams(vmem_limit_bytes=42 * MIB),
        cost_estimate=SMALL,
        name="settle",
    )(slots, returned)


def local(kv_part, queries, w_out, d_out, nbr_owner, nbr_slot):
    dp_count = lax.axis_size("dp")
    count = lax.axis_size("tensor")
    reader = lax.axis_index("dp")
    me = lax.axis_index("tensor")
    tokens, head_width = queries.shape
    share_width = 2 * head_width
    span_count = tokens // SPAN
    read_count = 2 * span_count
    out_width = d_out.shape[1]

    owner_ids = jnp.arange(dp_count, dtype=jnp.int32)
    per_reader = (nbr_owner[:, :, None] == owner_ids[None, None, :]).reshape(
        dp_count, read_count, dp_count
    )
    slot_from = jnp.max(
        jnp.where(per_reader, nbr_slot.reshape(dp_count, read_count, 1), 0), axis=1
    )
    owners = lax.dynamic_slice_in_dim(nbr_owner, reader * span_count, span_count, 0).reshape(
        read_count
    )
    slots = lax.dynamic_slice_in_dim(nbr_slot, reader * span_count, span_count, 0).reshape(
        read_count
    )
    ids = owners * NB_DEV + slots
    serving_slot = lax.dynamic_index_in_dim(slot_from, reader, 1, False)

    def kv_term(shard, received):
        total = lax.dynamic_slice_in_dim(
            kv_part[0], shard * share_width, share_width, 1
        ).astype(jnp.float32)
        for r in received:
            total = total + r.astype(jnp.float32)
        return total.astype(jnp.bfloat16)

    if count == 4:
        across = send(d_out, ACROSS)
        outwards = send(d_out, OUTWARDS)
        line = LineSum(kv_term, me)
        line.add_far(across, outwards)
        line.add_near(line.far_in)
        share = line.finish()
        two_in = send(after(d_out, line.near_sum), TWO_IN)
        inwards = send(after(d_out, two_in), INWARDS)
        groups = [
            (entry(range(4), me), [d_out]),
            (entry(NEAR, me), [across, send(after(across, line.near_sum), OUTWARDS)]),
            (entry(BESIDE, me), [inwards, outwards]),
            (entry(FAR, me), [two_in, send(two_in, OUTWARDS)]),
        ]
    else:
        share = lax.psum_scatter(kv_part[0], "tensor", scatter_dimension=1, tiled=True)
        gathered = lax.all_gather(d_out, "tensor", axis=0)
        groups = [(jnp.int32(s), [gathered[s]]) for s in range(count)]
    blocks = lax.all_gather(
        share.reshape(NB_DEV, NBR_LEN, share_width), "dp", axis=0, tiled=True
    )

    def mixed_term(shard, received):
        return project(shard, [attended], w_out, out_width, received)

    if count == 4:
        grads = back_project(groups[:1], w_out, None, jnp.float32)
        attended = attend(after(ids, grads), queries, blocks, 0)
        line = LineSum(mixed_term, me)
        first = (after(groups[1][0], line.beside), groups[1][1])
        grads = back_project([first] + groups[2:], w_out, grads, jnp.bfloat16)
        own_sums = attend_grad(ids, owners, dp_count, queries, grads, [blocks])
        line.add_far(own_sums)
        line.add_near(line.far_in)
        mixed = line.finish()
    else:
        attended = attend(ids, queries, blocks, 0)
        partial = jnp.concatenate(
            [mixed_term(jnp.int32(s), []) for s in range(count)], axis=1
        )
        mixed = lax.psum_scatter(partial, "tensor", scatter_dimension=1, tiled=True)
        grads = None
        for at in range(count):
            last = at == count - 1
            grads = back_project(
                groups[at : at + 1], w_out, grads, jnp.bfloat16 if last else jnp.float32
            )
        own_sums = attend_grad(ids, owners, dp_count, queries, grads, [blocks])
    returned = lax.all_to_all(own_sums, "dp", split_axis=0, concat_axis=0, tiled=True)
    return (mixed, settle(serving_slot, returned))


def solution(mesh):
    placed = (
        P("tensor", "dp", None),
        P("dp", "tensor"),
        P("tensor", None),
        P("dp", "tensor"),
        P(),
        P(),
    )
    return jax.shard_map(
        local,
        mesh=mesh,
        in_specs=placed,
        out_specs=(P("dp", "tensor"), P("dp", "tensor")),
        check_vma=False,
    )
```

```python
import functools

import jax
import jax.numpy as jnp
from jax import lax
from jax.experimental import pallas as pl
from jax.experimental.pallas import tpu as pltpu
from jax.sharding import PartitionSpec as P

HD = 128
SPAN = 64
NBR_LEN = 128
NB_DEV = 2
NT = (((1,), (1,)), ((), ()))
MIB = 1024 * 1024
SMALL = pl.CostEstimate(flops=1, bytes_accessed=1, transcendentals=0)


def pair_of(first, second, column):
    return jnp.concatenate(
        [first[0, :, column : column + HD], second[0, :, column : column + HD]], axis=0
    )


def two_heads_of(first, second, head, offset):
    left, right = 2 * head * HD + offset, 2 * (head + 1) * HD + offset
    rows = [
        jnp.concatenate([ref[0, :, left : left + HD], ref[0, :, right : right + HD]], axis=1)
        for ref in (first, second)
    ]
    return jnp.concatenate(rows, axis=0)


def block_diagonal(ref, rows, head):
    left = ref[rows, head * HD : (head + 1) * HD]
    right = ref[rows, (head + 1) * HD : (head + 2) * HD]
    blank = jnp.zeros_like(left)
    return jnp.concatenate(
        [jnp.concatenate([left, blank], axis=1), jnp.concatenate([blank, right], axis=1)], axis=0
    )


def attend_kernel(heads, ids_ref, q_ref, *refs):
    del ids_ref
    out_ref = refs[-1]
    every = [(c, h) for c in range(len(refs) // 2) for h in range(heads)]
    rows = [slice(c * SPAN, (c + 1) * SPAN) for c, _ in every]
    scores = [
        lax.dot_general(
            q_ref[r, h * HD : (h + 1) * HD],
            pair_of(refs[2 * c], refs[2 * c + 1], 2 * h * HD),
            NT,
            preferred_element_type=jnp.float32,
        )
        for r, (c, h) in zip(rows, every)
    ]
    highest = [jnp.max(s, axis=1, keepdims=True) for s in scores]
    expo = [jnp.exp((s - m) * (HD**-0.5)) for s, m in zip(scores, highest)]
    inverse = [1.0 / jnp.sum(e, axis=1, keepdims=True) for e in expo]
    probs = [(e * r).astype(jnp.bfloat16) for e, r in zip(expo, inverse)]
    for p, r, (c, h) in zip(probs, rows, every):
        values = pair_of(refs[2 * c], refs[2 * c + 1], 2 * h * HD + HD)
        out = jnp.dot(p, values, preferred_element_type=jnp.float32)
        out_ref[r, h * HD : (h + 1) * HD] = out.astype(jnp.bfloat16)


def neighbour_specs(group, share):
    def spec(place):
        return pl.BlockSpec(
            (1, NBR_LEN, share), lambda c, ids, *_: (ids[2 * group * c + place], 0, 0)
        )

    return [spec(place) for place in range(2 * group)]


def attend(ids, queries, blocks, part):
    tokens = queries.shape[0]
    spans = tokens // SPAN
    share = blocks.shape[2]
    width = share // 2
    group = 2 if spans % 2 == 0 else 1
    return pl.pallas_call(
        functools.partial(attend_kernel, width // HD),
        grid_spec=pltpu.PrefetchScalarGridSpec(
            num_scalar_prefetch=1,
            grid=(spans // group,),
            in_specs=[pl.BlockSpec((group * SPAN, width), lambda c, ids: (c, part))]
            + neighbour_specs(group, share),
            out_specs=pl.BlockSpec((group * SPAN, width), lambda c, ids: (c, 0)),
        ),
        out_shape=jax.ShapeDtypeStruct((tokens, width), jnp.bfloat16),
        compiler_params=pltpu.CompilerParams(vmem_limit_bytes=42 * MIB),
        cost_estimate=SMALL,
        name="attend",
    )(ids, queries, *([blocks] * (2 * group)))


def attend_grad_kernel(group, parts, ids_ref, own_ref, q_ref, g_ref, *refs):
    del ids_ref
    out_ref, total_ref = refs[-2:]
    step = pl.program_id(0)

    @pl.when(step == 0)
    def _():
        total_ref[...] = jnp.zeros_like(total_ref)

    factor = HD**-0.5
    heads = q_ref.shape[1] // HD
    part_heads = heads // parts
    for c in range(group):
        tokens = slice(c * SPAN, (c + 1) * SPAN)
        places = (
            (own_ref[2 * (group * step + c)], slice(0, NBR_LEN)),
            (own_ref[2 * (group * step + c) + 1], slice(NBR_LEN, 2 * NBR_LEN)),
        )
        for part in range(parts):
            first_ref, second_ref = refs[2 * (group * part + c) : 2 * (group * part + c) + 2]
            pairs = range(0, part_heads, 2)
            query = [block_diagonal(q_ref, tokens, part * part_heads + h) for h in pairs]
            grad = [block_diagonal(g_ref, tokens, part * part_heads + h) for h in pairs]
            scores = [
                lax.dot_general(
                    two_heads_of(first_ref, second_ref, h, 0),
                    x,
                    NT,
                    preferred_element_type=jnp.float32,
                )
                for h, x in zip(pairs, query)
            ]
            grad_probs = [
                lax.dot_general(
                    two_heads_of(first_ref, second_ref, h, HD),
                    x,
                    NT,
                    preferred_element_type=jnp.float32,
                )
                for h, x in zip(pairs, grad)
            ]
            highest = [jnp.max(s, axis=0, keepdims=True) for s in scores]
            expo = [jnp.exp((s - m) * factor) for s, m in zip(scores, highest)]
            inverse = [1.0 / jnp.sum(e, axis=0, keepdims=True) for e in expo]
            probs = [e * r for e, r in zip(expo, inverse)]
            inner = [jnp.sum(p * d, axis=0, keepdims=True) for p, d in zip(probs, grad_probs)]
            grad_scores = [
                (p * (d - i)).astype(jnp.bfloat16) for p, d, i in zip(probs, grad_probs, inner)
            ]
            grad_keys = [
                jnp.dot(d, x, preferred_element_type=jnp.float32)
                for d, x in zip(grad_scores, query)
            ]
            grad_values = [
                jnp.dot(p.astype(jnp.bfloat16), x, preferred_element_type=jnp.float32)
                for p, x in zip(probs, grad)
            ]
            for h, keys, values in zip(pairs, grad_keys, grad_values):
                for i in range(2):
                    at = 2 * (part * part_heads + h + i) * HD
                    lanes = slice(i * HD, (i + 1) * HD)
                    for owner, rows in places:
                        total_ref[owner, :, at : at + HD] += keys[rows, lanes]
                        total_ref[owner, :, at + HD : at + 2 * HD] += values[rows, lanes]

    @pl.when(step == pl.num_programs(0) - 1)
    def _():
        for h in range(heads):
            at = 2 * h * HD
            out_ref[:, :, at : at + HD] = (total_ref[:, :, at : at + HD] * factor).astype(
                jnp.bfloat16
            )
            out_ref[:, :, at + HD : at + 2 * HD] = total_ref[
                :, :, at + HD : at + 2 * HD
            ].astype(jnp.bfloat16)


def attend_grad(ids, owners, owner_count, queries, grads, blocks):
    tokens, width = queries.shape
    spans = tokens // SPAN
    parts = len(blocks)
    part_share = blocks[0].shape[2]
    share = parts * part_share
    group = 2 if spans % 2 == 0 else 1
    return pl.pallas_call(
        functools.partial(attend_grad_kernel, group, parts),
        grid_spec=pltpu.PrefetchScalarGridSpec(
            num_scalar_prefetch=2,
            grid=(spans // group,),
            in_specs=[pl.BlockSpec((group * SPAN, width), lambda c, ids, own: (c, 0))] * 2
            + neighbour_specs(group, part_share) * parts,
            out_specs=pl.BlockSpec(
                (owner_count, NBR_LEN, share), lambda c, ids, own: (0, 0, 0)
            ),
            scratch_shapes=[pltpu.VMEM((owner_count, NBR_LEN, share), jnp.float32)],
        ),
        out_shape=jax.ShapeDtypeStruct((owner_count, NBR_LEN, share), jnp.bfloat16),
        compiler_params=pltpu.CompilerParams(vmem_limit_bytes=50 * MIB),
        cost_estimate=SMALL,
        name="attend_grad",
    )(ids, owners, queries, grads, *[b for b in blocks for _ in range(2 * group)])


def tile_of(width):
    return next(tile for tile in (512, 384, 256, HD) if width % tile == 0)


def project_kernel(parts, received, shard_ref, *refs):
    del shard_ref
    inputs, weights = refs[:parts], refs[parts : 2 * parts]
    total = jnp.dot(inputs[0][...], weights[0][...], preferred_element_type=jnp.float32)
    for x, w in zip(inputs[1:], weights[1:]):
        total = total + jnp.dot(x[...], w[...], preferred_element_type=jnp.float32)
    for r in refs[2 * parts : 2 * parts + received]:
        total = total + r[...].astype(jnp.float32)
    refs[-1][...] = total.astype(jnp.bfloat16)


def project(shard, inputs, w_out, width, received):
    parts = len(inputs)
    tokens, depth = inputs[0].shape
    tile = tile_of(width)
    steps = width // tile

    def weights_of(part):
        return pl.BlockSpec((depth, tile), lambda j, s: (part, s[0] * steps + j))

    return pl.pallas_call(
        functools.partial(project_kernel, parts, len(received)),
        grid_spec=pltpu.PrefetchScalarGridSpec(
            num_scalar_prefetch=1,
            grid=(steps,),
            in_specs=[pl.BlockSpec((tokens, depth), lambda j, s: (0, 0))] * parts
            + [weights_of(part) for part in range(parts)]
            + [pl.BlockSpec((tokens, tile), lambda j, s: (0, j))] * len(received),
            out_specs=pl.BlockSpec((tokens, tile), lambda j, s: (0, j)),
        ),
        out_shape=jax.ShapeDtypeStruct((tokens, width), jnp.bfloat16),
        compiler_params=pltpu.CompilerParams(vmem_limit_bytes=42 * MIB),
        cost_estimate=SMALL,
        name="project",
    )(shard.reshape(1), *inputs, *([w_out] * parts), *received)


def back_project_kernel(counts, carried, shards_ref, *refs):
    del shards_ref
    weights, out_ref = refs[: len(counts)], refs[-1]
    total = refs[-2][...] if carried else None
    at = len(counts)
    for count, weight in zip(counts, weights):
        block = refs[at][...]
        for other in refs[at + 1 : at + count]:
            block = block + other[...]
        at += count
        term = lax.dot_general(block, weight[...], NT, preferred_element_type=jnp.float32)
        total = term if total is None else total + term
    out_ref[...] = total.astype(out_ref.dtype)


def back_project(groups, w_out, carry, out_type):
    tokens, depth = groups[0][1][0].shape
    head_width = w_out.shape[0]
    tile = tile_of(head_width)
    blocks = [block for _, sources in groups for block in sources]
    extra = [] if carry is None else [carry]

    def weights_of(group):
        return pl.BlockSpec((tile, depth), lambda j, s: (j, s[group]))

    return pl.pallas_call(
        functools.partial(
            back_project_kernel, [len(sources) for _, sources in groups], carry is not None
        ),
        grid_spec=pltpu.PrefetchScalarGridSpec(
            num_scalar_prefetch=1,
            grid=(head_width // tile,),
            in_specs=[weights_of(group) for group in range(len(groups))]
            + [pl.BlockSpec((tokens, depth), lambda j, s: (0, 0), pipeline_mode=pl.Buffered(1))]
            * len(blocks)
            + [pl.BlockSpec((tokens, tile), lambda j, s: (0, j))] * len(extra),
            out_specs=pl.BlockSpec((tokens, tile), lambda j, s: (0, j)),
        ),
        out_shape=jax.ShapeDtypeStruct((tokens, head_width), out_type),
        compiler_params=pltpu.CompilerParams(vmem_limit_bytes=48 * MIB),
        cost_estimate=SMALL,
        name="back_project",
    )(jnp.stack([shard for shard, _ in groups]), *([w_out] * len(groups)), *blocks, *extra)


def after(x, *others):
    return lax.optimization_barrier((x, *others))[0]


INWARDS = [(0, 1), (3, 2)]
OUTWARDS = [(1, 0), (2, 3)]
SWAP = [(0, 1), (1, 0), (2, 3), (3, 2)]
ACROSS = [(1, 2), (2, 1)]
TWO_ON = [(1, 3), (2, 0)]
TWO_IN = [(3, 1), (0, 2)]


def send(x, hops):
    return lax.ppermute(x, "tensor", hops)


def far_of(me):
    return jnp.where(me < 2, 3, 0)


def near_of(me):
    return jnp.where(me < 2, 2, 1)


def beside_of(me):
    return me ^ 1


def sum_kernel(*refs):
    total = refs[0][...].astype(jnp.float32)
    for ref in refs[1:-1]:
        total = total + ref[...].astype(jnp.float32)
    refs[-1][...] = total.astype(jnp.bfloat16)


def sum_of(arrays):
    rows, width = arrays[0].shape
    steps = 2 if rows % 32 == 0 else 1
    block = pl.BlockSpec((rows // steps, width), lambda j: (j, 0))
    return pl.pallas_call(
        sum_kernel,
        grid=(steps,),
        in_specs=[block] * len(arrays),
        out_specs=block,
        out_shape=jax.ShapeDtypeStruct((rows, width), jnp.bfloat16),
        compiler_params=pltpu.CompilerParams(vmem_limit_bytes=42 * MIB),
        cost_estimate=SMALL,
        name="sum_of",
    )(*arrays)


class LineSum:
    def __init__(self, term, me):
        self.term, self.me = term, me
        self.far = term(far_of(me), [])
        self.far_in = send(self.far, INWARDS)
        self.near = term(after(near_of(me), self.far), [])
        self.near_in = send(self.near, INWARDS)

    def add_beside(self, *others):
        self.beside = self.term(after(beside_of(self.me), self.near, *others), [])
        self.beside_in = send(self.beside, SWAP)

    def add_far(self, *others):
        self.far_sum = sum_of([self.far, after(self.far_in, *others)])
        self.far_in = send(self.far_sum, TWO_ON)

    def add_near(self, *others):
        self.near_sum = sum_of([self.near, after(self.near_in, *others)])
        self.near_in = send(self.near_sum, ACROSS)

    def received(self):
        return [self.beside_in, self.far_in, self.near_in]

    def finish(self, *others):
        return self.term(after(self.me, *others), self.received())


def settle_kernel(slot_ref, returned_ref, out_ref):
    totals = [jnp.zeros(returned_ref.shape[1:], jnp.float32) for _ in range(NB_DEV)]
    for r in range(returned_ref.shape[0]):
        block = returned_ref[r].astype(jnp.float32)
        for slot in range(NB_DEV):
            totals[slot] = totals[slot] + jnp.where(slot_ref[r] == slot, block, 0.0)
    for slot in range(NB_DEV):
        out_ref[slot * NBR_LEN : (slot + 1) * NBR_LEN] = totals[slot].astype(jnp.bfloat16)


def settle(slots, returned):
    readers, _, width = returned.shape
    tile = next(tile for tile in (1024, 768, 512, 256, HD) if width % tile == 0)
    return pl.pallas_call(
        settle_kernel,
        grid_spec=pltpu.PrefetchScalarGridSpec(
            num_scalar_prefetch=1,
            grid=(width // tile,),
            in_specs=[pl.BlockSpec((readers, NBR_LEN, tile), lambda j, s: (0, 0, j))],
            out_specs=pl.BlockSpec((NB_DEV * NBR_LEN, tile), lambda j, s: (0, j)),
        ),
        out_shape=jax.ShapeDtypeStruct((NB_DEV * NBR_LEN, width), jnp.bfloat16),
        compiler_params=pltpu.CompilerParams(vmem_limit_bytes=42 * MIB),
        cost_estimate=SMALL,
        name="settle",
    )(slots, returned)


def local(kv_part, queries, w_out, d_out, nbr_owner, nbr_slot):
    dp_count = lax.axis_size("dp")
    count = lax.axis_size("tensor")
    reader = lax.axis_index("dp")
    me = lax.axis_index("tensor")
    tokens, head_width = queries.shape
    share_width = 2 * head_width
    span_count = tokens // SPAN
    read_count = 2 * span_count
    out_width = d_out.shape[1]

    owner_ids = jnp.arange(dp_count, dtype=jnp.int32)
    per_reader = (nbr_owner[:, :, None] == owner_ids[None, None, :]).reshape(
        dp_count, read_count, dp_count
    )
    slot_from = jnp.max(
        jnp.where(per_reader, nbr_slot.reshape(dp_count, read_count, 1), 0), axis=1
    )
    owners = lax.dynamic_slice_in_dim(nbr_owner, reader * span_count, span_count, 0).reshape(
        read_count
    )
    slots = lax.dynamic_slice_in_dim(nbr_slot, reader * span_count, span_count, 0).reshape(
        read_count
    )
    ids = owners * NB_DEV + slots
    serving_slot = lax.dynamic_index_in_dim(slot_from, reader, 1, False)

    def kv_term(shard, received):
        term = lax.dynamic_slice_in_dim(kv_part[0], shard * share_width, share_width, 1)
        return sum_of([term, *received]) if received else term

    if count == 4:
        across = send(d_out, ACROSS)
        outwards = send(d_out, OUTWARDS)
        line = LineSum(kv_term, me)
        line.add_beside()
        line.add_far(across, outwards)
        line.add_near(line.far_in)
        share = line.finish()
        two_in = send(after(d_out, line.near_sum), TWO_IN)
        inwards = send(after(d_out, two_in), INWARDS)
        groups = [
            (me, [d_out]),
            (near_of(me), [across, send(after(across, line.near_sum), OUTWARDS)]),
            (beside_of(me), [inwards, outwards]),
            (far_of(me), [two_in, send(two_in, OUTWARDS)]),
        ]
    else:
        share = lax.psum_scatter(kv_part[0], "tensor", scatter_dimension=1, tiled=True)
        gathered = lax.all_gather(d_out, "tensor", axis=0)
        groups = [(jnp.int32(s), [gathered[s]]) for s in range(count)]
    blocks = lax.all_gather(
        share.reshape(NB_DEV, NBR_LEN, share_width), "dp", axis=0, tiled=True
    )

    def mixed_term(shard, received):
        return project(shard, [attended], w_out, out_width, received)

    if count == 4:
        grads = back_project(groups[:1], w_out, None, jnp.float32)
        attended = attend(after(ids, grads), queries, blocks, 0)
        line = LineSum(mixed_term, me)
        first = (after(groups[1][0], line.near), groups[1][1])
        grads = back_project([first] + groups[2:], w_out, grads, jnp.bfloat16)
        own_sums = attend_grad(ids, owners, dp_count, queries, grads, [blocks])
        line.add_far(own_sums)
        line.add_beside(line.far_sum)
        mine = mixed_term(after(me, line.beside), [])
        line.add_near(line.far_in, mine)
    else:
        attended = attend(ids, queries, blocks, 0)
        partial = jnp.concatenate(
            [mixed_term(jnp.int32(s), []) for s in range(count)], axis=1
        )
        mixed = lax.psum_scatter(partial, "tensor", scatter_dimension=1, tiled=True)
        grads = None
        for at in range(count):
            last = at == count - 1
            grads = back_project(
                groups[at : at + 1], w_out, grads, jnp.bfloat16 if last else jnp.float32
            )
        own_sums = attend_grad(ids, owners, dp_count, queries, grads, [blocks])
    returned = lax.all_to_all(own_sums, "dp", split_axis=0, concat_axis=0, tiled=True)
    d_kv = settle(serving_slot, returned)
    if count == 4:
        mixed = sum_of([after(mine, d_kv), *line.received()])
    return (mixed, d_kv)


def solution(mesh):
    placed = (
        P("tensor", "dp", None),
        P("dp", "tensor"),
        P("tensor", None),
        P("dp", "tensor"),
        P(),
        P(),
    )
    return jax.shard_map(
        local,
        mesh=mesh,
        in_specs=placed,
        out_specs=(P("dp", "tensor"), P("dp", "tensor")),
        check_vma=False,
    )
```

```python
import functools

import jax
import jax.numpy as jnp
from jax import lax
from jax.experimental import pallas as pl
from jax.experimental.pallas import tpu as pltpu
from jax.sharding import PartitionSpec as P

HD = 128
SPAN = 64
NBR_LEN = 128
NB_DEV = 2
NT = (((1,), (1,)), ((), ()))
MIB = 1024 * 1024
SMALL = pl.CostEstimate(flops=1, bytes_accessed=1, transcendentals=0)


def pair_of(first, second, column):
    return jnp.concatenate(
        [first[0, :, column : column + HD], second[0, :, column : column + HD]], axis=0
    )


def two_heads_of(first, second, head, offset):
    left, right = 2 * head * HD + offset, 2 * (head + 1) * HD + offset
    rows = [
        jnp.concatenate([ref[0, :, left : left + HD], ref[0, :, right : right + HD]], axis=1)
        for ref in (first, second)
    ]
    return jnp.concatenate(rows, axis=0)


def block_diagonal(ref, rows, head):
    left = ref[rows, head * HD : (head + 1) * HD]
    right = ref[rows, (head + 1) * HD : (head + 2) * HD]
    blank = jnp.zeros_like(left)
    return jnp.concatenate(
        [jnp.concatenate([left, blank], axis=1), jnp.concatenate([blank, right], axis=1)], axis=0
    )


def attend_kernel(heads, ids_ref, q_ref, *refs):
    del ids_ref
    out_ref = refs[-1]
    every = [(c, h) for c in range(len(refs) // 2) for h in range(heads)]
    rows = [slice(c * SPAN, (c + 1) * SPAN) for c, _ in every]
    scores = [
        lax.dot_general(
            q_ref[r, h * HD : (h + 1) * HD],
            pair_of(refs[2 * c], refs[2 * c + 1], 2 * h * HD),
            NT,
            preferred_element_type=jnp.float32,
        )
        for r, (c, h) in zip(rows, every)
    ]
    highest = [jnp.max(s, axis=1, keepdims=True) for s in scores]
    expo = [jnp.exp((s - m) * (HD**-0.5)) for s, m in zip(scores, highest)]
    inverse = [1.0 / jnp.sum(e, axis=1, keepdims=True) for e in expo]
    probs = [(e * r).astype(jnp.bfloat16) for e, r in zip(expo, inverse)]
    for p, r, (c, h) in zip(probs, rows, every):
        values = pair_of(refs[2 * c], refs[2 * c + 1], 2 * h * HD + HD)
        out = jnp.dot(p, values, preferred_element_type=jnp.float32)
        out_ref[r, h * HD : (h + 1) * HD] = out.astype(jnp.bfloat16)


def neighbour_specs(group, share, part):
    def spec(place):
        return pl.BlockSpec(
            (1, NBR_LEN, share), lambda c, ids, *_: (ids[2 * group * c + place], 0, part)
        )

    return [spec(place) for place in range(2 * group)]


def attend(ids, queries, blocks, part):
    tokens = queries.shape[0]
    spans = tokens // SPAN
    share = blocks.shape[2]
    width = share // 2
    group = 2 if spans % 2 == 0 else 1
    return pl.pallas_call(
        functools.partial(attend_kernel, width // HD),
        grid_spec=pltpu.PrefetchScalarGridSpec(
            num_scalar_prefetch=1,
            grid=(spans // group,),
            in_specs=[pl.BlockSpec((group * SPAN, width), lambda c, ids: (c, part))]
            + neighbour_specs(group, share, 0),
            out_specs=pl.BlockSpec((group * SPAN, width), lambda c, ids: (c, 0)),
        ),
        out_shape=jax.ShapeDtypeStruct((tokens, width), jnp.bfloat16),
        compiler_params=pltpu.CompilerParams(vmem_limit_bytes=42 * MIB),
        cost_estimate=SMALL,
        name="attend",
    )(ids, queries, *([blocks] * (2 * group)))


def attend_grad_kernel(group, ids_ref, own_ref, q_ref, g_ref, *refs):
    del ids_ref
    out_ref, total_ref = refs[-2:]
    step = pl.program_id(0)

    @pl.when(step == 0)
    def _():
        total_ref[...] = jnp.zeros_like(total_ref)

    factor = HD**-0.5
    heads = q_ref.shape[1] // HD
    for c in range(group):
        tokens = slice(c * SPAN, (c + 1) * SPAN)
        places = (
            (own_ref[2 * (group * step + c)], slice(0, NBR_LEN)),
            (own_ref[2 * (group * step + c) + 1], slice(NBR_LEN, 2 * NBR_LEN)),
        )
        first_ref, second_ref = refs[2 * c : 2 * c + 2]
        pairs = range(0, heads, 2)
        query = [block_diagonal(q_ref, tokens, h) for h in pairs]
        grad = [block_diagonal(g_ref, tokens, h) for h in pairs]
        scores = [
            lax.dot_general(
                two_heads_of(first_ref, second_ref, h, 0),
                x,
                NT,
                preferred_element_type=jnp.float32,
            )
            for h, x in zip(pairs, query)
        ]
        grad_probs = [
            lax.dot_general(
                two_heads_of(first_ref, second_ref, h, HD),
                x,
                NT,
                preferred_element_type=jnp.float32,
            )
            for h, x in zip(pairs, grad)
        ]
        highest = [jnp.max(s, axis=0, keepdims=True) for s in scores]
        expo = [jnp.exp((s - m) * factor) for s, m in zip(scores, highest)]
        inverse = [1.0 / jnp.sum(e, axis=0, keepdims=True) for e in expo]
        probs = [e * r for e, r in zip(expo, inverse)]
        inner = [jnp.sum(p * d, axis=0, keepdims=True) for p, d in zip(probs, grad_probs)]
        grad_scores = [
            (p * (d - i)).astype(jnp.bfloat16) for p, d, i in zip(probs, grad_probs, inner)
        ]
        grad_keys = [
            jnp.dot(d, x, preferred_element_type=jnp.float32)
            for d, x in zip(grad_scores, query)
        ]
        grad_values = [
            jnp.dot(p.astype(jnp.bfloat16), x, preferred_element_type=jnp.float32)
            for p, x in zip(probs, grad)
        ]
        for h, keys, values in zip(pairs, grad_keys, grad_values):
            for i in range(2):
                at = 2 * (h + i) * HD
                lanes = slice(i * HD, (i + 1) * HD)
                for owner, rows in places:
                    total_ref[owner, :, at : at + HD] += keys[rows, lanes]
                    total_ref[owner, :, at + HD : at + 2 * HD] += values[rows, lanes]

    @pl.when(step == pl.num_programs(0) - 1)
    def _():
        for h in range(heads):
            at = 2 * h * HD
            out_ref[:, :, at : at + HD] = (total_ref[:, :, at : at + HD] * factor).astype(
                jnp.bfloat16
            )
            out_ref[:, :, at + HD : at + 2 * HD] = total_ref[
                :, :, at + HD : at + 2 * HD
            ].astype(jnp.bfloat16)


def attend_grad(ids, owners, owner_count, queries, grads, blocks, part, parts):
    tokens = queries.shape[0]
    spans = tokens // SPAN
    width, share = queries.shape[1] // parts, blocks.shape[2] // parts
    group = 2 if spans % 2 == 0 else 1
    return pl.pallas_call(
        functools.partial(attend_grad_kernel, group),
        grid_spec=pltpu.PrefetchScalarGridSpec(
            num_scalar_prefetch=2,
            grid=(spans // group,),
            in_specs=[pl.BlockSpec((group * SPAN, width), lambda c, ids, own: (c, part))] * 2
            + neighbour_specs(group, share, part),
            out_specs=pl.BlockSpec(
                (owner_count, NBR_LEN, share), lambda c, ids, own: (0, 0, 0)
            ),
            scratch_shapes=[pltpu.VMEM((owner_count, NBR_LEN, share), jnp.float32)],
        ),
        out_shape=jax.ShapeDtypeStruct((owner_count, NBR_LEN, share), jnp.bfloat16),
        compiler_params=pltpu.CompilerParams(vmem_limit_bytes=48 * MIB),
        cost_estimate=SMALL,
        name="attend_grad",
    )(ids, owners, queries, grads, *([blocks] * (2 * group)))


def tile_of(width):
    return next(tile for tile in (512, 384, 256, HD) if width % tile == 0)


def project_kernel(parts, received, shard_ref, *refs):
    del shard_ref
    inputs, weights = refs[:parts], refs[parts : 2 * parts]
    total = jnp.dot(inputs[0][...], weights[0][...], preferred_element_type=jnp.float32)
    for x, w in zip(inputs[1:], weights[1:]):
        total = total + jnp.dot(x[...], w[...], preferred_element_type=jnp.float32)
    for r in refs[2 * parts : 2 * parts + received]:
        total = total + r[...].astype(jnp.float32)
    refs[-1][...] = total.astype(jnp.bfloat16)


def project(shard, inputs, w_out, width, received):
    parts = len(inputs)
    tokens, depth = inputs[0].shape
    tile = tile_of(width)
    steps = width // tile

    def weights_of(part):
        return pl.BlockSpec((depth, tile), lambda j, s: (part, s[0] * steps + j))

    return pl.pallas_call(
        functools.partial(project_kernel, parts, len(received)),
        grid_spec=pltpu.PrefetchScalarGridSpec(
            num_scalar_prefetch=1,
            grid=(steps,),
            in_specs=[pl.BlockSpec((tokens, depth), lambda j, s: (0, 0))] * parts
            + [weights_of(part) for part in range(parts)]
            + [pl.BlockSpec((tokens, tile), lambda j, s: (0, j))] * len(received),
            out_specs=pl.BlockSpec((tokens, tile), lambda j, s: (0, j)),
        ),
        out_shape=jax.ShapeDtypeStruct((tokens, width), jnp.bfloat16),
        compiler_params=pltpu.CompilerParams(vmem_limit_bytes=42 * MIB),
        cost_estimate=SMALL,
        name="project",
    )(shard.reshape(1), *inputs, *([w_out] * parts), *received)


def back_project_kernel(counts, carried, shards_ref, *refs):
    del shards_ref
    weights, out_ref = refs[: len(counts)], refs[-1]
    total = refs[-2][...] if carried else None
    at = len(counts)
    for count, weight in zip(counts, weights):
        block = refs[at][...]
        for other in refs[at + 1 : at + count]:
            block = block + other[...]
        at += count
        term = lax.dot_general(block, weight[...], NT, preferred_element_type=jnp.float32)
        total = term if total is None else total + term
    out_ref[...] = total.astype(out_ref.dtype)


def back_project(groups, w_out, carry, out_type):
    tokens, depth = groups[0][1][0].shape
    head_width = w_out.shape[0]
    tile = tile_of(head_width)
    blocks = [block for _, sources in groups for block in sources]
    extra = [] if carry is None else [carry]

    def weights_of(group):
        return pl.BlockSpec((tile, depth), lambda j, s: (j, s[group]))

    return pl.pallas_call(
        functools.partial(
            back_project_kernel, [len(sources) for _, sources in groups], carry is not None
        ),
        grid_spec=pltpu.PrefetchScalarGridSpec(
            num_scalar_prefetch=1,
            grid=(head_width // tile,),
            in_specs=[weights_of(group) for group in range(len(groups))]
            + [pl.BlockSpec((tokens, depth), lambda j, s: (0, 0), pipeline_mode=pl.Buffered(1))]
            * len(blocks)
            + [pl.BlockSpec((tokens, tile), lambda j, s: (0, j))] * len(extra),
            out_specs=pl.BlockSpec((tokens, tile), lambda j, s: (0, j)),
        ),
        out_shape=jax.ShapeDtypeStruct((tokens, head_width), out_type),
        compiler_params=pltpu.CompilerParams(vmem_limit_bytes=48 * MIB),
        cost_estimate=SMALL,
        name="back_project",
    )(jnp.stack([shard for shard, _ in groups]), *([w_out] * len(groups)), *blocks, *extra)


def after(x, *others):
    return lax.optimization_barrier((x, *others))[0]


INWARDS = [(0, 1), (3, 2)]
OUTWARDS = [(1, 0), (2, 3)]
SWAP = [(0, 1), (1, 0), (2, 3), (3, 2)]
ACROSS = [(1, 2), (2, 1)]
TWO_ON = [(1, 3), (2, 0)]
TWO_IN = [(3, 1), (0, 2)]


def send(x, hops):
    return lax.ppermute(x, "tensor", hops)


def far_of(me):
    return jnp.where(me < 2, 3, 0)


def near_of(me):
    return jnp.where(me < 2, 2, 1)


def beside_of(me):
    return me ^ 1


def sum_kernel(*refs):
    total = refs[0][...].astype(jnp.float32)
    for ref in refs[1:-1]:
        total = total + ref[...].astype(jnp.float32)
    refs[-1][...] = total.astype(jnp.bfloat16)


def sum_of(arrays):
    rows, width = arrays[0].shape
    steps = 2 if rows % 32 == 0 else 1
    block = pl.BlockSpec((rows // steps, width), lambda j: (j, 0))
    return pl.pallas_call(
        sum_kernel,
        grid=(steps,),
        in_specs=[block] * len(arrays),
        out_specs=block,
        out_shape=jax.ShapeDtypeStruct((rows, width), jnp.bfloat16),
        compiler_params=pltpu.CompilerParams(vmem_limit_bytes=42 * MIB),
        cost_estimate=SMALL,
        name="sum_of",
    )(*arrays)


class LineSum:
    def __init__(self, term, me):
        self.term, self.me = term, me
        self.far = term(far_of(me), [])
        self.far_in = send(self.far, INWARDS)
        self.near = term(after(near_of(me), self.far), [])
        self.near_in = send(self.near, INWARDS)

    def add_beside(self, *others):
        self.beside = self.term(after(beside_of(self.me), self.near, *others), [])

    def swap_beside(self, *others):
        self.beside_in = send(after(self.beside, *others), SWAP)

    def add_far(self, *others):
        self.far_sum = sum_of([self.far, after(self.far_in, *others)])
        self.far_in = send(self.far_sum, TWO_ON)

    def add_near(self, *others):
        self.near_sum = sum_of([self.near, after(self.near_in, *others)])
        self.near_in = send(self.near_sum, ACROSS)

    def received(self):
        return [self.beside_in, self.far_in, self.near_in]

    def finish(self, *others):
        return self.term(after(self.me, *others), self.received())


def settle_kernel(steps, slot_ref, *refs):
    for part, returned_ref in enumerate(refs[:-1]):

        @pl.when(pl.program_id(0) // steps == part)
        def _(returned_ref=returned_ref):
            totals = [jnp.zeros(returned_ref.shape[1:], jnp.float32) for _ in range(NB_DEV)]
            for r in range(returned_ref.shape[0]):
                block = returned_ref[r].astype(jnp.float32)
                for slot in range(NB_DEV):
                    totals[slot] = totals[slot] + jnp.where(slot_ref[r] == slot, block, 0.0)
            for slot in range(NB_DEV):
                rows = slice(slot * NBR_LEN, (slot + 1) * NBR_LEN)
                refs[-1][rows] = totals[slot].astype(jnp.bfloat16)


def settle(slots, returned):
    readers, _, width = returned[0].shape
    tile = next(tile for tile in (768, 512, 256, HD) if width % tile == 0)
    steps = width // tile

    def spec(part):
        return pl.BlockSpec(
            (readers, NBR_LEN, tile),
            lambda j, s: (0, 0, jnp.clip(j - part * steps, 0, steps - 1)),
        )

    return pl.pallas_call(
        functools.partial(settle_kernel, steps),
        grid_spec=pltpu.PrefetchScalarGridSpec(
            num_scalar_prefetch=1,
            grid=(len(returned) * steps,),
            in_specs=[spec(part) for part in range(len(returned))],
            out_specs=pl.BlockSpec((NB_DEV * NBR_LEN, tile), lambda j, s: (0, j)),
        ),
        out_shape=jax.ShapeDtypeStruct((NB_DEV * NBR_LEN, len(returned) * width), jnp.bfloat16),
        compiler_params=pltpu.CompilerParams(vmem_limit_bytes=42 * MIB),
        cost_estimate=SMALL,
        name="settle",
    )(slots, *returned)


def local(kv_part, queries, w_out, d_out, nbr_owner, nbr_slot):
    dp_count = lax.axis_size("dp")
    count = lax.axis_size("tensor")
    reader = lax.axis_index("dp")
    me = lax.axis_index("tensor")
    tokens, head_width = queries.shape
    share_width = 2 * head_width
    span_count = tokens // SPAN
    read_count = 2 * span_count
    out_width = d_out.shape[1]

    owner_ids = jnp.arange(dp_count, dtype=jnp.int32)
    per_reader = (nbr_owner[:, :, None] == owner_ids[None, None, :]).reshape(
        dp_count, read_count, dp_count
    )
    slot_from = jnp.max(
        jnp.where(per_reader, nbr_slot.reshape(dp_count, read_count, 1), 0), axis=1
    )
    owners = lax.dynamic_slice_in_dim(nbr_owner, reader * span_count, span_count, 0).reshape(
        read_count
    )
    slots = lax.dynamic_slice_in_dim(nbr_slot, reader * span_count, span_count, 0).reshape(
        read_count
    )
    ids = owners * NB_DEV + slots
    serving_slot = lax.dynamic_index_in_dim(slot_from, reader, 1, False)

    def kv_term(shard, received):
        term = lax.dynamic_slice_in_dim(kv_part[0], shard * share_width, share_width, 1)
        return sum_of([term, *received]) if received else term

    if count == 4:
        across = send(d_out, ACROSS)
        outwards = send(d_out, OUTWARDS)
        line = LineSum(kv_term, me)
        line.add_beside()
        line.swap_beside()
        line.add_far(across, outwards)
        line.add_near(line.far_in)
        share = line.finish()
        two_in = send(after(d_out, line.near_sum), TWO_IN)
        grads = back_project([(after(me, share), [d_out])], w_out, None, jnp.float32)
        inwards = send(after(d_out, grads), INWARDS)
        groups = [
            (me, [d_out]),
            (near_of(me), [across, send(after(across, line.near_sum), OUTWARDS)]),
            (beside_of(me), [inwards, outwards]),
            (far_of(me), [two_in, send(two_in, OUTWARDS)]),
        ]
    else:
        share = lax.psum_scatter(kv_part[0], "tensor", scatter_dimension=1, tiled=True)
        gathered = lax.all_gather(d_out, "tensor", axis=0)
        groups = [(jnp.int32(s), [gathered[s]]) for s in range(count)]
    blocks = lax.all_gather(
        share.reshape(NB_DEV, NBR_LEN, share_width), "dp", axis=0, tiled=True
    )

    parts = 2 if (head_width // HD) % 4 == 0 else 1

    def grad_part(ids, part):
        return attend_grad(ids, owners, dp_count, queries, grads, blocks, part, parts)

    def mixed_term(shard, received):
        return project(shard, [attended], w_out, out_width, received)

    if count == 4:
        near = (after(groups[1][0], two_in), groups[1][1])
        grads = back_project([near], w_out, grads, jnp.float32)
        attended = attend(after(ids, grads), queries, blocks, 0)
        line = LineSum(mixed_term, me)
        first = (after(groups[2][0], line.near), groups[2][1])
        grads = back_project([first] + groups[3:], w_out, grads, jnp.bfloat16)
        own_sums = [grad_part(ids, 0)]
        line.add_far(own_sums[0])
        own_sums.append(grad_part(after(ids, line.far_sum), 1))
        line.add_beside(own_sums[1])
        line.swap_beside(line.near_in)
        mine = mixed_term(after(me, line.beside), [])
        own_sums[1] = after(own_sums[1], mine)
        line.add_near(line.far_in, mine)
    else:
        attended = attend(ids, queries, blocks, 0)
        partial = jnp.concatenate(
            [mixed_term(jnp.int32(s), []) for s in range(count)], axis=1
        )
        mixed = lax.psum_scatter(partial, "tensor", scatter_dimension=1, tiled=True)
        grads = None
        for at in range(count):
            last = at == count - 1
            grads = back_project(
                groups[at : at + 1], w_out, grads, jnp.bfloat16 if last else jnp.float32
            )
        own_sums = [grad_part(ids, part) for part in range(parts)]
    returned = [
        lax.all_to_all(part, "dp", split_axis=0, concat_axis=0, tiled=True) for part in own_sums
    ]
    d_kv = settle(serving_slot, returned)
    if count == 4:
        mine = sum_of([after(mine, d_kv), line.beside_in, line.far_in])
        mixed = sum_of([mine, line.near_in])
    return (mixed, d_kv)


def solution(mesh):
    placed = (
        P("tensor", "dp", None),
        P("dp", "tensor"),
        P("tensor", None),
        P("dp", "tensor"),
        P(),
        P(),
    )
    return jax.shard_map(
        local,
        mesh=mesh,
        in_specs=placed,
        out_specs=(P("dp", "tensor"), P("dp", "tensor")),
        check_vma=False,
    )
```

```python
import functools

import jax
import jax.numpy as jnp
from jax import lax
from jax.experimental import pallas as pl
from jax.experimental.pallas import tpu as pltpu
from jax.sharding import PartitionSpec as P

HD = 128
SPAN = 64
NBR_LEN = 128
NB_DEV = 2
NT = (((1,), (1,)), ((), ()))
MIB = 1024 * 1024
SMALL = pl.CostEstimate(flops=1, bytes_accessed=1, transcendentals=0)


def pair_of(first, second, column):
    return jnp.concatenate(
        [first[0, :, column : column + HD], second[0, :, column : column + HD]], axis=0
    )


def two_heads_of(first, second, head, offset):
    left, right = 2 * head * HD + offset, 2 * (head + 1) * HD + offset
    rows = [
        jnp.concatenate([ref[0, :, left : left + HD], ref[0, :, right : right + HD]], axis=1)
        for ref in (first, second)
    ]
    return jnp.concatenate(rows, axis=0)


def block_diagonal(ref, rows, head):
    left = ref[rows, head * HD : (head + 1) * HD]
    right = ref[rows, (head + 1) * HD : (head + 2) * HD]
    blank = jnp.zeros_like(left)
    return jnp.concatenate(
        [jnp.concatenate([left, blank], axis=1), jnp.concatenate([blank, right], axis=1)], axis=0
    )


def attend_kernel(heads, ids_ref, q_ref, *refs):
    del ids_ref
    out_ref = refs[-1]
    every = [(c, h) for c in range(len(refs) // 2) for h in range(heads)]
    rows = [slice(c * SPAN, (c + 1) * SPAN) for c, _ in every]
    scores = [
        lax.dot_general(
            q_ref[r, h * HD : (h + 1) * HD],
            pair_of(refs[2 * c], refs[2 * c + 1], 2 * h * HD),
            NT,
            preferred_element_type=jnp.float32,
        )
        for r, (c, h) in zip(rows, every)
    ]
    highest = [jnp.max(s, axis=1, keepdims=True) for s in scores]
    expo = [jnp.exp((s - m) * (HD**-0.5)) for s, m in zip(scores, highest)]
    inverse = [1.0 / jnp.sum(e, axis=1, keepdims=True) for e in expo]
    probs = [(e * r).astype(jnp.bfloat16) for e, r in zip(expo, inverse)]
    for p, r, (c, h) in zip(probs, rows, every):
        values = pair_of(refs[2 * c], refs[2 * c + 1], 2 * h * HD + HD)
        out = jnp.dot(p, values, preferred_element_type=jnp.float32)
        out_ref[r, h * HD : (h + 1) * HD] = out.astype(jnp.bfloat16)


def neighbour_specs(group, share, part):
    def spec(place):
        return pl.BlockSpec(
            (1, NBR_LEN, share), lambda c, ids, *_: (ids[2 * group * c + place], 0, part)
        )

    return [spec(place) for place in range(2 * group)]


def attend(ids, queries, blocks, part):
    tokens = queries.shape[0]
    spans = tokens // SPAN
    share = blocks.shape[2]
    width = share // 2
    group = 2 if spans % 2 == 0 else 1
    return pl.pallas_call(
        functools.partial(attend_kernel, width // HD),
        grid_spec=pltpu.PrefetchScalarGridSpec(
            num_scalar_prefetch=1,
            grid=(spans // group,),
            in_specs=[pl.BlockSpec((group * SPAN, width), lambda c, ids: (c, part))]
            + neighbour_specs(group, share, 0),
            out_specs=pl.BlockSpec((group * SPAN, width), lambda c, ids: (c, 0)),
        ),
        out_shape=jax.ShapeDtypeStruct((tokens, width), jnp.bfloat16),
        compiler_params=pltpu.CompilerParams(vmem_limit_bytes=42 * MIB),
        cost_estimate=SMALL,
        name="attend",
    )(ids, queries, *([blocks] * (2 * group)))


def attend_grad_kernel(group, ids_ref, own_ref, q_ref, g_ref, *refs):
    del ids_ref
    out_ref, total_ref = refs[-2:]
    step = pl.program_id(0)

    @pl.when(step == 0)
    def _():
        total_ref[...] = jnp.zeros_like(total_ref)

    factor = HD**-0.5
    heads = q_ref.shape[1] // HD
    for c in range(group):
        tokens = slice(c * SPAN, (c + 1) * SPAN)
        places = (
            (own_ref[2 * (group * step + c)], slice(0, NBR_LEN)),
            (own_ref[2 * (group * step + c) + 1], slice(NBR_LEN, 2 * NBR_LEN)),
        )
        first_ref, second_ref = refs[2 * c : 2 * c + 2]
        pairs = range(0, heads, 2)
        query = [block_diagonal(q_ref, tokens, h) for h in pairs]
        grad = [block_diagonal(g_ref, tokens, h) for h in pairs]
        scores = [
            lax.dot_general(
                two_heads_of(first_ref, second_ref, h, 0),
                x,
                NT,
                preferred_element_type=jnp.float32,
            )
            for h, x in zip(pairs, query)
        ]
        grad_probs = [
            lax.dot_general(
                two_heads_of(first_ref, second_ref, h, HD),
                x,
                NT,
                preferred_element_type=jnp.float32,
            )
            for h, x in zip(pairs, grad)
        ]
        highest = [jnp.max(s, axis=0, keepdims=True) for s in scores]
        expo = [jnp.exp((s - m) * factor) for s, m in zip(scores, highest)]
        inverse = [1.0 / jnp.sum(e, axis=0, keepdims=True) for e in expo]
        probs = [e * r for e, r in zip(expo, inverse)]
        inner = [jnp.sum(p * d, axis=0, keepdims=True) for p, d in zip(probs, grad_probs)]
        grad_scores = [
            (p * (d - i)).astype(jnp.bfloat16) for p, d, i in zip(probs, grad_probs, inner)
        ]
        grad_keys = [
            jnp.dot(d, x, preferred_element_type=jnp.float32)
            for d, x in zip(grad_scores, query)
        ]
        grad_values = [
            jnp.dot(p.astype(jnp.bfloat16), x, preferred_element_type=jnp.float32)
            for p, x in zip(probs, grad)
        ]
        for h, keys, values in zip(pairs, grad_keys, grad_values):
            for i in range(2):
                at = 2 * (h + i) * HD
                lanes = slice(i * HD, (i + 1) * HD)
                for owner, rows in places:
                    total_ref[owner, :, at : at + HD] += keys[rows, lanes]
                    total_ref[owner, :, at + HD : at + 2 * HD] += values[rows, lanes]

    @pl.when(step == pl.num_programs(0) - 1)
    def _():
        for h in range(heads):
            at = 2 * h * HD
            out_ref[:, :, at : at + HD] = (total_ref[:, :, at : at + HD] * factor).astype(
                jnp.bfloat16
            )
            out_ref[:, :, at + HD : at + 2 * HD] = total_ref[
                :, :, at + HD : at + 2 * HD
            ].astype(jnp.bfloat16)


def attend_grad(ids, owners, owner_count, queries, grads, blocks, part, parts):
    tokens = queries.shape[0]
    spans = tokens // SPAN
    width, share = queries.shape[1] // parts, blocks.shape[2] // parts
    group = 2 if spans % 2 == 0 else 1
    return pl.pallas_call(
        functools.partial(attend_grad_kernel, group),
        grid_spec=pltpu.PrefetchScalarGridSpec(
            num_scalar_prefetch=2,
            grid=(spans // group,),
            in_specs=[pl.BlockSpec((group * SPAN, width), lambda c, ids, own: (c, part))] * 2
            + neighbour_specs(group, share, part),
            out_specs=pl.BlockSpec(
                (owner_count, NBR_LEN, share), lambda c, ids, own: (0, 0, 0)
            ),
            scratch_shapes=[pltpu.VMEM((owner_count, NBR_LEN, share), jnp.float32)],
        ),
        out_shape=jax.ShapeDtypeStruct((owner_count, NBR_LEN, share), jnp.bfloat16),
        compiler_params=pltpu.CompilerParams(vmem_limit_bytes=48 * MIB),
        cost_estimate=SMALL,
        name="attend_grad",
    )(ids, owners, queries, grads, *([blocks] * (2 * group)))


def tile_of(width):
    return next(tile for tile in (512, 384, 256, HD) if width % tile == 0)


def project_kernel(parts, received, shard_ref, *refs):
    del shard_ref
    inputs, weights = refs[:parts], refs[parts : 2 * parts]
    total = jnp.dot(inputs[0][...], weights[0][...], preferred_element_type=jnp.float32)
    for x, w in zip(inputs[1:], weights[1:]):
        total = total + jnp.dot(x[...], w[...], preferred_element_type=jnp.float32)
    for r in refs[2 * parts : 2 * parts + received]:
        total = total + r[...].astype(jnp.float32)
    refs[-1][...] = total.astype(jnp.bfloat16)


def project(shard, inputs, w_out, width, received):
    parts = len(inputs)
    tokens, depth = inputs[0].shape
    tile = tile_of(width)
    steps = width // tile

    def weights_of(part):
        return pl.BlockSpec((depth, tile), lambda j, s: (part, s[0] * steps + j))

    return pl.pallas_call(
        functools.partial(project_kernel, parts, len(received)),
        grid_spec=pltpu.PrefetchScalarGridSpec(
            num_scalar_prefetch=1,
            grid=(steps,),
            in_specs=[pl.BlockSpec((tokens, depth), lambda j, s: (0, 0))] * parts
            + [weights_of(part) for part in range(parts)]
            + [pl.BlockSpec((tokens, tile), lambda j, s: (0, j))] * len(received),
            out_specs=pl.BlockSpec((tokens, tile), lambda j, s: (0, j)),
        ),
        out_shape=jax.ShapeDtypeStruct((tokens, width), jnp.bfloat16),
        compiler_params=pltpu.CompilerParams(vmem_limit_bytes=42 * MIB),
        cost_estimate=SMALL,
        name="project",
    )(shard.reshape(1), *inputs, *([w_out] * parts), *received)


def back_project_kernel(counts, carried, shards_ref, *refs):
    del shards_ref
    weights, out_ref = refs[: len(counts)], refs[-1]
    total = refs[-2][...] if carried else None
    at = len(counts)
    for count, weight in zip(counts, weights):
        block = refs[at][...]
        for other in refs[at + 1 : at + count]:
            block = block + other[...]
        at += count
        term = lax.dot_general(block, weight[...], NT, preferred_element_type=jnp.float32)
        total = term if total is None else total + term
    out_ref[...] = total.astype(out_ref.dtype)


def back_project(groups, w_out, carry, out_type):
    tokens, depth = groups[0][1][0].shape
    head_width = w_out.shape[0]
    tile = tile_of(head_width)
    blocks = [block for _, sources in groups for block in sources]
    extra = [] if carry is None else [carry]

    def weights_of(group):
        return pl.BlockSpec((tile, depth), lambda j, s: (j, s[group]))

    return pl.pallas_call(
        functools.partial(
            back_project_kernel, [len(sources) for _, sources in groups], carry is not None
        ),
        grid_spec=pltpu.PrefetchScalarGridSpec(
            num_scalar_prefetch=1,
            grid=(head_width // tile,),
            in_specs=[weights_of(group) for group in range(len(groups))]
            + [pl.BlockSpec((tokens, depth), lambda j, s: (0, 0), pipeline_mode=pl.Buffered(1))]
            * len(blocks)
            + [pl.BlockSpec((tokens, tile), lambda j, s: (0, j))] * len(extra),
            out_specs=pl.BlockSpec((tokens, tile), lambda j, s: (0, j)),
        ),
        out_shape=jax.ShapeDtypeStruct((tokens, head_width), out_type),
        compiler_params=pltpu.CompilerParams(vmem_limit_bytes=48 * MIB),
        cost_estimate=SMALL,
        name="back_project",
    )(jnp.stack([shard for shard, _ in groups]), *([w_out] * len(groups)), *blocks, *extra)


def after(x, *others):
    return lax.optimization_barrier((x, *others))[0]


INWARDS = [(0, 1), (3, 2)]
OUTWARDS = [(1, 0), (2, 3)]
SWAP = [(0, 1), (1, 0), (2, 3), (3, 2)]
ACROSS = [(1, 2), (2, 1)]
TWO_ON = [(1, 3), (2, 0)]
TWO_IN = [(3, 1), (0, 2)]


def send(x, hops):
    return lax.ppermute(x, "tensor", hops)


def far_of(me):
    return jnp.where(me < 2, 3, 0)


def near_of(me):
    return jnp.where(me < 2, 2, 1)


def beside_of(me):
    return me ^ 1


def sum_kernel(*refs):
    total = refs[0][...].astype(jnp.float32)
    for ref in refs[1:-1]:
        total = total + ref[...].astype(jnp.float32)
    refs[-1][...] = total.astype(jnp.bfloat16)


def sum_of(arrays):
    rows, width = arrays[0].shape
    steps = 2 if rows % 32 == 0 else 1
    block = pl.BlockSpec((rows // steps, width), lambda j: (j, 0))
    return pl.pallas_call(
        sum_kernel,
        grid=(steps,),
        in_specs=[block] * len(arrays),
        out_specs=block,
        out_shape=jax.ShapeDtypeStruct((rows, width), jnp.bfloat16),
        compiler_params=pltpu.CompilerParams(vmem_limit_bytes=42 * MIB),
        cost_estimate=SMALL,
        name="sum_of",
    )(*arrays)


class LineSum:
    def __init__(self, term, me):
        self.term, self.me = term, me
        self.far = term(far_of(me), [])
        self.far_in = send(self.far, INWARDS)
        self.near = term(after(near_of(me), self.far), [])
        self.near_in = send(self.near, INWARDS)

    def add_beside(self, *others):
        self.beside = self.term(after(beside_of(self.me), self.near, *others), [])

    def swap_beside(self, *others):
        self.beside_in = send(after(self.beside, *others), SWAP)

    def add_far(self, *others):
        self.far_sum = sum_of([self.far, after(self.far_in, *others)])
        self.far_in = send(self.far_sum, TWO_ON)

    def add_near(self, *others):
        self.near_sum = sum_of([self.near, after(self.near_in, *others)])
        self.near_in = send(self.near_sum, ACROSS)

    def received(self):
        return [self.beside_in, self.far_in, self.near_in]

    def finish(self, *others):
        return self.term(after(self.me, *others), self.received())


def settle_kernel(steps, slot_ref, *refs):
    for part, returned_ref in enumerate(refs[:-1]):

        @pl.when(pl.program_id(0) // steps == part)
        def _(returned_ref=returned_ref):
            totals = [jnp.zeros(returned_ref.shape[1:], jnp.float32) for _ in range(NB_DEV)]
            for r in range(returned_ref.shape[0]):
                block = returned_ref[r].astype(jnp.float32)
                for slot in range(NB_DEV):
                    totals[slot] = totals[slot] + jnp.where(slot_ref[r] == slot, block, 0.0)
            for slot in range(NB_DEV):
                rows = slice(slot * NBR_LEN, (slot + 1) * NBR_LEN)
                refs[-1][rows] = totals[slot].astype(jnp.bfloat16)


def settle(slots, returned):
    readers, _, width = returned[0].shape
    tile = next(tile for tile in (768, 512, 256, HD) if width % tile == 0)
    steps = width // tile

    def spec(part):
        return pl.BlockSpec(
            (readers, NBR_LEN, tile),
            lambda j, s: (0, 0, jnp.clip(j - part * steps, 0, steps - 1)),
        )

    return pl.pallas_call(
        functools.partial(settle_kernel, steps),
        grid_spec=pltpu.PrefetchScalarGridSpec(
            num_scalar_prefetch=1,
            grid=(len(returned) * steps,),
            in_specs=[spec(part) for part in range(len(returned))],
            out_specs=pl.BlockSpec((NB_DEV * NBR_LEN, tile), lambda j, s: (0, j)),
        ),
        out_shape=jax.ShapeDtypeStruct((NB_DEV * NBR_LEN, len(returned) * width), jnp.bfloat16),
        compiler_params=pltpu.CompilerParams(vmem_limit_bytes=42 * MIB),
        cost_estimate=SMALL,
        name="settle",
    )(slots, *returned)


def local(kv_part, queries, w_out, d_out, nbr_owner, nbr_slot):
    dp_count = lax.axis_size("dp")
    count = lax.axis_size("tensor")
    reader = lax.axis_index("dp")
    me = lax.axis_index("tensor")
    tokens, head_width = queries.shape
    share_width = 2 * head_width
    span_count = tokens // SPAN
    read_count = 2 * span_count
    out_width = d_out.shape[1]

    owner_ids = jnp.arange(dp_count, dtype=jnp.int32)
    per_reader = (nbr_owner[:, :, None] == owner_ids[None, None, :]).reshape(
        dp_count, read_count, dp_count
    )
    slot_from = jnp.max(
        jnp.where(per_reader, nbr_slot.reshape(dp_count, read_count, 1), 0), axis=1
    )
    owners = lax.dynamic_slice_in_dim(nbr_owner, reader * span_count, span_count, 0).reshape(
        read_count
    )
    slots = lax.dynamic_slice_in_dim(nbr_slot, reader * span_count, span_count, 0).reshape(
        read_count
    )
    ids = owners * NB_DEV + slots
    serving_slot = lax.dynamic_index_in_dim(slot_from, reader, 1, False)

    parts = 2 if (head_width // HD) % 4 == 0 else 1
    by_line = count == 4 and parts == 2

    def kv_term(shard, received):
        term = lax.dynamic_slice_in_dim(kv_part[0], shard * share_width, share_width, 1)
        return sum_of([term, *received]) if received else term

    if by_line:
        outwards = send(d_out, OUTWARDS)
        line = LineSum(kv_term, me)
        across = send(after(d_out, line.far), ACROSS)
        line.add_far(outwards)
        line.add_beside(across)
        line.swap_beside()
        line.add_near(line.far_in)
        share = line.finish()
        two_in = send(after(d_out, line.near_sum), TWO_IN)
        grads = back_project([(after(me, share), [d_out])], w_out, None, jnp.float32)
        inwards = send(after(d_out, grads), INWARDS)
        groups = [
            (me, [d_out]),
            (near_of(me), [across, send(after(across, line.near_sum), OUTWARDS)]),
            (beside_of(me), [inwards, outwards]),
            (far_of(me), [two_in, send(two_in, OUTWARDS)]),
        ]
    else:
        share = lax.psum_scatter(kv_part[0], "tensor", scatter_dimension=1, tiled=True)
        gathered = lax.all_gather(d_out, "tensor", axis=0)
        groups = [(jnp.int32(s), [gathered[s]]) for s in range(count)]
    blocks = lax.all_gather(
        share.reshape(NB_DEV, NBR_LEN, share_width), "dp", axis=0, tiled=True
    )

    def grad_part(ids, part):
        return attend_grad(ids, owners, dp_count, queries, grads, blocks, part, parts)

    def mixed_term(shard, received):
        return project(shard, [attended], w_out, out_width, received)

    if by_line:
        near = (after(groups[1][0], two_in), groups[1][1])
        grads = back_project([near], w_out, grads, jnp.float32)
        attended = attend(after(ids, grads), queries, blocks, 0)
        line = LineSum(mixed_term, me)
        first = (after(groups[2][0], line.near), groups[2][1])
        grads = back_project([first] + groups[3:], w_out, grads, jnp.bfloat16)
        own_sums = [grad_part(ids, 0)]
        line.add_far(own_sums[0])
        own_sums.append(grad_part(after(ids, line.far_sum), 1))
        line.add_beside(own_sums[1])
        line.swap_beside(line.near_in)
        mine = mixed_term(after(me, line.beside), [])
        own_sums[1] = after(own_sums[1], mine)
        line.add_near(line.far_in, mine)
    else:
        attended = attend(ids, queries, blocks, 0)
        partial = jnp.concatenate(
            [mixed_term(jnp.int32(s), []) for s in range(count)], axis=1
        )
        mixed = lax.psum_scatter(partial, "tensor", scatter_dimension=1, tiled=True)
        grads = None
        for at in range(count):
            last = at == count - 1
            grads = back_project(
                groups[at : at + 1], w_out, grads, jnp.bfloat16 if last else jnp.float32
            )
        own_sums = [grad_part(ids, part) for part in range(parts)]
    returned = [
        lax.all_to_all(part, "dp", split_axis=0, concat_axis=0, tiled=True) for part in own_sums
    ]
    d_kv = settle(serving_slot, returned)
    if by_line:
        mine = sum_of([after(mine, d_kv), line.beside_in, line.far_in])
        mixed = sum_of([mine, line.near_in])
    return (mixed, d_kv)


def solution(mesh):
    placed = (
        P("tensor", "dp", None),
        P("dp", "tensor"),
        P("tensor", None),
        P("dp", "tensor"),
        P(),
        P(),
    )
    return jax.shard_map(
        local,
        mesh=mesh,
        in_specs=placed,
        out_specs=(P("dp", "tensor"), P("dp", "tensor")),
        check_vma=False,
    )
```

```python
import functools

import jax
import jax.numpy as jnp
from jax import lax
from jax.experimental import pallas as pl
from jax.experimental.pallas import tpu as pltpu
from jax.sharding import PartitionSpec as P

HD = 128
SPAN = 64
NBR_LEN = 128
NB_DEV = 2
NT = (((1,), (1,)), ((), ()))
MIB = 1024 * 1024
SMALL = pl.CostEstimate(flops=1, bytes_accessed=1, transcendentals=0)


def pair_of(first, second, column):
    return jnp.concatenate(
        [first[0, :, column : column + HD], second[0, :, column : column + HD]], axis=0
    )


def two_heads_of(first, second, head, offset):
    left, right = 2 * head * HD + offset, 2 * (head + 1) * HD + offset
    rows = [
        jnp.concatenate([ref[0, :, left : left + HD], ref[0, :, right : right + HD]], axis=1)
        for ref in (first, second)
    ]
    return jnp.concatenate(rows, axis=0)


def block_diagonal(ref, rows, head):
    left = ref[rows, head * HD : (head + 1) * HD]
    right = ref[rows, (head + 1) * HD : (head + 2) * HD]
    blank = jnp.zeros_like(left)
    return jnp.concatenate(
        [jnp.concatenate([left, blank], axis=1), jnp.concatenate([blank, right], axis=1)], axis=0
    )


def attend_kernel(heads, ids_ref, q_ref, *refs):
    del ids_ref
    out_ref = refs[-1]
    every = [(c, h) for c in range(len(refs) // 2) for h in range(heads)]
    rows = [slice(c * SPAN, (c + 1) * SPAN) for c, _ in every]
    scores = [
        lax.dot_general(
            q_ref[r, h * HD : (h + 1) * HD],
            pair_of(refs[2 * c], refs[2 * c + 1], 2 * h * HD),
            NT,
            preferred_element_type=jnp.float32,
        )
        for r, (c, h) in zip(rows, every)
    ]
    highest = [jnp.max(s, axis=1, keepdims=True) for s in scores]
    expo = [jnp.exp((s - m) * (HD**-0.5)) for s, m in zip(scores, highest)]
    inverse = [1.0 / jnp.sum(e, axis=1, keepdims=True) for e in expo]
    probs = [(e * r).astype(jnp.bfloat16) for e, r in zip(expo, inverse)]
    for p, r, (c, h) in zip(probs, rows, every):
        values = pair_of(refs[2 * c], refs[2 * c + 1], 2 * h * HD + HD)
        out = jnp.dot(p, values, preferred_element_type=jnp.float32)
        out_ref[r, h * HD : (h + 1) * HD] = out.astype(jnp.bfloat16)


def neighbour_specs(group, share, part):
    def spec(place):
        return pl.BlockSpec(
            (1, NBR_LEN, share), lambda c, ids, *_: (ids[2 * group * c + place], 0, part)
        )

    return [spec(place) for place in range(2 * group)]


def attend(ids, queries, blocks, part):
    tokens = queries.shape[0]
    spans = tokens // SPAN
    share = blocks.shape[2]
    width = share // 2
    group = 2 if spans % 2 == 0 else 1
    return pl.pallas_call(
        functools.partial(attend_kernel, width // HD),
        grid_spec=pltpu.PrefetchScalarGridSpec(
            num_scalar_prefetch=1,
            grid=(spans // group,),
            in_specs=[pl.BlockSpec((group * SPAN, width), lambda c, ids: (c, part))]
            + neighbour_specs(group, share, 0),
            out_specs=pl.BlockSpec((group * SPAN, width), lambda c, ids: (c, 0)),
        ),
        out_shape=jax.ShapeDtypeStruct((tokens, width), jnp.bfloat16),
        compiler_params=pltpu.CompilerParams(vmem_limit_bytes=42 * MIB),
        cost_estimate=SMALL,
        name="attend",
    )(ids, queries, *([blocks] * (2 * group)))


def attend_grad_kernel(group, ids_ref, own_ref, q_ref, g_ref, *refs):
    del ids_ref
    out_ref, total_ref = refs[-2:]
    step = pl.program_id(0)

    @pl.when(step == 0)
    def _():
        total_ref[...] = jnp.zeros_like(total_ref)

    factor = HD**-0.5
    heads = q_ref.shape[1] // HD
    for c in range(group):
        tokens = slice(c * SPAN, (c + 1) * SPAN)
        places = (
            (own_ref[2 * (group * step + c)], slice(0, NBR_LEN)),
            (own_ref[2 * (group * step + c) + 1], slice(NBR_LEN, 2 * NBR_LEN)),
        )
        first_ref, second_ref = refs[2 * c : 2 * c + 2]
        pairs = range(0, heads, 2)
        query = [block_diagonal(q_ref, tokens, h) for h in pairs]
        grad = [block_diagonal(g_ref, tokens, h) for h in pairs]
        scores = [
            lax.dot_general(
                two_heads_of(first_ref, second_ref, h, 0),
                x,
                NT,
                preferred_element_type=jnp.float32,
            )
            for h, x in zip(pairs, query)
        ]
        grad_probs = [
            lax.dot_general(
                two_heads_of(first_ref, second_ref, h, HD),
                x,
                NT,
                preferred_element_type=jnp.float32,
            )
            for h, x in zip(pairs, grad)
        ]
        highest = [jnp.max(s, axis=0, keepdims=True) for s in scores]
        expo = [jnp.exp((s - m) * factor) for s, m in zip(scores, highest)]
        inverse = [1.0 / jnp.sum(e, axis=0, keepdims=True) for e in expo]
        probs = [e * r for e, r in zip(expo, inverse)]
        inner = [jnp.sum(p * d, axis=0, keepdims=True) for p, d in zip(probs, grad_probs)]
        grad_scores = [
            (p * (d - i)).astype(jnp.bfloat16) for p, d, i in zip(probs, grad_probs, inner)
        ]
        grad_keys = [
            jnp.dot(d, x, preferred_element_type=jnp.float32)
            for d, x in zip(grad_scores, query)
        ]
        grad_values = [
            jnp.dot(p.astype(jnp.bfloat16), x, preferred_element_type=jnp.float32)
            for p, x in zip(probs, grad)
        ]
        for h, keys, values in zip(pairs, grad_keys, grad_values):
            for i in range(2):
                at = 2 * (h + i) * HD
                lanes = slice(i * HD, (i + 1) * HD)
                for owner, rows in places:
                    total_ref[owner, :, at : at + HD] += keys[rows, lanes]
                    total_ref[owner, :, at + HD : at + 2 * HD] += values[rows, lanes]

    @pl.when(step == pl.num_programs(0) - 1)
    def _():
        for h in range(heads):
            at = 2 * h * HD
            out_ref[:, :, at : at + HD] = (total_ref[:, :, at : at + HD] * factor).astype(
                jnp.bfloat16
            )
            out_ref[:, :, at + HD : at + 2 * HD] = total_ref[
                :, :, at + HD : at + 2 * HD
            ].astype(jnp.bfloat16)


def attend_grad(ids, owners, owner_count, queries, grads, blocks, part, parts):
    tokens = queries.shape[0]
    spans = tokens // SPAN
    width, share = queries.shape[1] // parts, blocks.shape[2] // parts
    group = 2 if spans % 2 == 0 else 1
    return pl.pallas_call(
        functools.partial(attend_grad_kernel, group),
        grid_spec=pltpu.PrefetchScalarGridSpec(
            num_scalar_prefetch=2,
            grid=(spans // group,),
            in_specs=[pl.BlockSpec((group * SPAN, width), lambda c, ids, own: (c, part))] * 2
            + neighbour_specs(group, share, part),
            out_specs=pl.BlockSpec(
                (owner_count, NBR_LEN, share), lambda c, ids, own: (0, 0, 0)
            ),
            scratch_shapes=[pltpu.VMEM((owner_count, NBR_LEN, share), jnp.float32)],
        ),
        out_shape=jax.ShapeDtypeStruct((owner_count, NBR_LEN, share), jnp.bfloat16),
        compiler_params=pltpu.CompilerParams(vmem_limit_bytes=48 * MIB),
        cost_estimate=SMALL,
        name="attend_grad",
    )(ids, owners, queries, grads, *([blocks] * (2 * group)))


def tile_of(width):
    return next(tile for tile in (1024, 768, 512, 384, 256, HD) if width % tile == 0)


def project_kernel(parts, received, shard_ref, *refs):
    del shard_ref
    inputs, weights = refs[:parts], refs[parts : 2 * parts]
    total = jnp.dot(inputs[0][...], weights[0][...], preferred_element_type=jnp.float32)
    for x, w in zip(inputs[1:], weights[1:]):
        total = total + jnp.dot(x[...], w[...], preferred_element_type=jnp.float32)
    for r in refs[2 * parts : 2 * parts + received]:
        total = total + r[...].astype(jnp.float32)
    refs[-1][...] = total.astype(jnp.bfloat16)


def project(shard, inputs, w_out, width, received):
    parts = len(inputs)
    tokens, depth = inputs[0].shape
    tile = tile_of(width)
    steps = width // tile

    def weights_of(part):
        return pl.BlockSpec((depth, tile), lambda j, s: (part, s[0] * steps + j))

    return pl.pallas_call(
        functools.partial(project_kernel, parts, len(received)),
        grid_spec=pltpu.PrefetchScalarGridSpec(
            num_scalar_prefetch=1,
            grid=(steps,),
            in_specs=[pl.BlockSpec((tokens, depth), lambda j, s: (0, 0))] * parts
            + [weights_of(part) for part in range(parts)]
            + [pl.BlockSpec((tokens, tile), lambda j, s: (0, j))] * len(received),
            out_specs=pl.BlockSpec((tokens, tile), lambda j, s: (0, j)),
        ),
        out_shape=jax.ShapeDtypeStruct((tokens, width), jnp.bfloat16),
        compiler_params=pltpu.CompilerParams(vmem_limit_bytes=42 * MIB),
        cost_estimate=SMALL,
        name="project",
    )(shard.reshape(1), *inputs, *([w_out] * parts), *received)


def back_project_kernel(counts, carried, shards_ref, *refs):
    del shards_ref
    weights, out_ref = refs[: len(counts)], refs[-1]
    total = refs[-2][...] if carried else None
    at = len(counts)
    for count, weight in zip(counts, weights):
        block = refs[at][...]
        for other in refs[at + 1 : at + count]:
            block = block + other[...]
        at += count
        term = lax.dot_general(block, weight[...], NT, preferred_element_type=jnp.float32)
        total = term if total is None else total + term
    out_ref[...] = total.astype(out_ref.dtype)


def back_project(groups, w_out, carry, out_type):
    tokens, depth = groups[0][1][0].shape
    head_width = w_out.shape[0]
    tile = tile_of(head_width)
    blocks = [block for _, sources in groups for block in sources]
    extra = [] if carry is None else [carry]

    def weights_of(group):
        return pl.BlockSpec((tile, depth), lambda j, s: (j, s[group]))

    return pl.pallas_call(
        functools.partial(
            back_project_kernel, [len(sources) for _, sources in groups], carry is not None
        ),
        grid_spec=pltpu.PrefetchScalarGridSpec(
            num_scalar_prefetch=1,
            grid=(head_width // tile,),
            in_specs=[weights_of(group) for group in range(len(groups))]
            + [pl.BlockSpec((tokens, depth), lambda j, s: (0, 0), pipeline_mode=pl.Buffered(1))]
            * len(blocks)
            + [pl.BlockSpec((tokens, tile), lambda j, s: (0, j))] * len(extra),
            out_specs=pl.BlockSpec((tokens, tile), lambda j, s: (0, j)),
        ),
        out_shape=jax.ShapeDtypeStruct((tokens, head_width), out_type),
        compiler_params=pltpu.CompilerParams(vmem_limit_bytes=48 * MIB),
        cost_estimate=SMALL,
        name="back_project",
    )(jnp.stack([shard for shard, _ in groups]), *([w_out] * len(groups)), *blocks, *extra)


def after(x, *others):
    return lax.optimization_barrier((x, *others))[0]


INWARDS = [(0, 1), (3, 2)]
OUTWARDS = [(1, 0), (2, 3)]
SWAP = [(0, 1), (1, 0), (2, 3), (3, 2)]
ACROSS = [(1, 2), (2, 1)]
TWO_ON = [(1, 3), (2, 0)]
TWO_IN = [(3, 1), (0, 2)]


def send(x, hops):
    return lax.ppermute(x, "tensor", hops)


def far_of(me):
    return jnp.where(me < 2, 3, 0)


def near_of(me):
    return jnp.where(me < 2, 2, 1)


def beside_of(me):
    return me ^ 1


def sum_kernel(*refs):
    total = refs[0][...].astype(jnp.float32)
    for ref in refs[1:-1]:
        total = total + ref[...].astype(jnp.float32)
    refs[-1][...] = total.astype(jnp.bfloat16)


def sum_of(arrays):
    rows, width = arrays[0].shape
    steps = 2 if rows % 32 == 0 else 1
    block = pl.BlockSpec((rows // steps, width), lambda j: (j, 0))
    return pl.pallas_call(
        sum_kernel,
        grid=(steps,),
        in_specs=[block] * len(arrays),
        out_specs=block,
        out_shape=jax.ShapeDtypeStruct((rows, width), jnp.bfloat16),
        compiler_params=pltpu.CompilerParams(vmem_limit_bytes=42 * MIB),
        cost_estimate=SMALL,
        name="sum_of",
    )(*arrays)


class LineSum:
    def __init__(self, term, me):
        self.term, self.me = term, me
        self.far = term(far_of(me), [])
        self.far_in = send(self.far, INWARDS)
        self.near = term(after(near_of(me), self.far), [])
        self.near_in = send(self.near, INWARDS)

    def add_beside(self, *others):
        self.beside = self.term(after(beside_of(self.me), self.near, *others), [])

    def swap_beside(self, *others):
        self.beside_in = send(after(self.beside, *others), SWAP)

    def add_far(self, *others):
        self.far_sum = sum_of([self.far, after(self.far_in, *others)])
        self.far_in = send(self.far_sum, TWO_ON)

    def add_near(self, *others):
        self.near_sum = sum_of([self.near, after(self.near_in, *others)])
        self.near_in = send(self.near_sum, ACROSS)

    def received(self):
        return [self.beside_in, self.far_in, self.near_in]

    def finish(self, *others):
        return self.term(after(self.me, *others), self.received())


def settle_kernel(steps, slot_ref, *refs):
    for part, returned_ref in enumerate(refs[:-1]):

        @pl.when(pl.program_id(0) // steps == part)
        def _(returned_ref=returned_ref):
            totals = [jnp.zeros(returned_ref.shape[1:], jnp.float32) for _ in range(NB_DEV)]
            for r in range(returned_ref.shape[0]):
                block = returned_ref[r].astype(jnp.float32)
                for slot in range(NB_DEV):
                    totals[slot] = totals[slot] + jnp.where(slot_ref[r] == slot, block, 0.0)
            for slot in range(NB_DEV):
                rows = slice(slot * NBR_LEN, (slot + 1) * NBR_LEN)
                refs[-1][rows] = totals[slot].astype(jnp.bfloat16)


def settle(slots, returned):
    readers, _, width = returned[0].shape
    tile = next(tile for tile in (768, 512, 256, HD) if width % tile == 0)
    steps = width // tile

    def spec(part):
        return pl.BlockSpec(
            (readers, NBR_LEN, tile),
            lambda j, s: (0, 0, jnp.clip(j - part * steps, 0, steps - 1)),
        )

    return pl.pallas_call(
        functools.partial(settle_kernel, steps),
        grid_spec=pltpu.PrefetchScalarGridSpec(
            num_scalar_prefetch=1,
            grid=(len(returned) * steps,),
            in_specs=[spec(part) for part in range(len(returned))],
            out_specs=pl.BlockSpec((NB_DEV * NBR_LEN, tile), lambda j, s: (0, j)),
        ),
        out_shape=jax.ShapeDtypeStruct((NB_DEV * NBR_LEN, len(returned) * width), jnp.bfloat16),
        compiler_params=pltpu.CompilerParams(vmem_limit_bytes=42 * MIB),
        cost_estimate=SMALL,
        name="settle",
    )(slots, *returned)


def local(kv_part, queries, w_out, d_out, nbr_owner, nbr_slot):
    dp_count = lax.axis_size("dp")
    count = lax.axis_size("tensor")
    reader = lax.axis_index("dp")
    me = lax.axis_index("tensor")
    tokens, head_width = queries.shape
    share_width = 2 * head_width
    span_count = tokens // SPAN
    read_count = 2 * span_count
    out_width = d_out.shape[1]

    owner_ids = jnp.arange(dp_count, dtype=jnp.int32)
    per_reader = (nbr_owner[:, :, None] == owner_ids[None, None, :]).reshape(
        dp_count, read_count, dp_count
    )
    slot_from = jnp.max(
        jnp.where(per_reader, nbr_slot.reshape(dp_count, read_count, 1), 0), axis=1
    )
    owners = lax.dynamic_slice_in_dim(nbr_owner, reader * span_count, span_count, 0).reshape(
        read_count
    )
    slots = lax.dynamic_slice_in_dim(nbr_slot, reader * span_count, span_count, 0).reshape(
        read_count
    )
    ids = owners * NB_DEV + slots
    serving_slot = lax.dynamic_index_in_dim(slot_from, reader, 1, False)

    parts = 2 if (head_width // HD) % 4 == 0 else 1
    by_line = count == 4 and parts == 2

    def kv_term(shard, received):
        term = lax.dynamic_slice_in_dim(kv_part[0], shard * share_width, share_width, 1)
        return sum_of([term, *received]) if received else term

    if by_line:
        outwards = send(d_out, OUTWARDS)
        line = LineSum(kv_term, me)
        across = send(after(d_out, line.far), ACROSS)
        line.add_far(outwards)
        line.add_beside(across)
        line.swap_beside()
        line.add_near(line.far_in)
        share = line.finish()
        two_in = send(after(d_out, line.near_sum), TWO_IN)
        grads = back_project([(after(me, share), [d_out])], w_out, None, jnp.float32)
        inwards = send(after(d_out, grads), INWARDS)
        groups = [
            (me, [d_out]),
            (near_of(me), [across, send(after(across, line.near_sum), OUTWARDS)]),
            (beside_of(me), [inwards, outwards]),
            (far_of(me), [two_in, send(two_in, OUTWARDS)]),
        ]
    else:
        share = lax.psum_scatter(kv_part[0], "tensor", scatter_dimension=1, tiled=True)
        gathered = lax.all_gather(d_out, "tensor", axis=0)
        groups = [(jnp.int32(s), [gathered[s]]) for s in range(count)]
    blocks = lax.all_gather(
        share.reshape(NB_DEV, NBR_LEN, share_width), "dp", axis=0, tiled=True
    )

    def grad_part(ids, part):
        return attend_grad(ids, owners, dp_count, queries, grads, blocks, part, parts)

    def mixed_term(shard, received):
        return project(shard, [attended], w_out, out_width, received)

    if by_line:
        near = (after(groups[1][0], two_in), groups[1][1])
        grads = back_project([near], w_out, grads, jnp.float32)
        attended = attend(after(ids, grads), queries, blocks, 0)
        line = LineSum(mixed_term, me)
        first = (after(groups[2][0], line.near), groups[2][1])
        grads = back_project([first] + groups[3:], w_out, grads, jnp.bfloat16)
        own_sums = [grad_part(ids, 0)]
        line.add_far(own_sums[0])
        own_sums.append(grad_part(after(ids, line.far_sum), 1))
        line.add_beside(own_sums[1])
        line.swap_beside(line.near_in)
        mine = mixed_term(after(me, line.beside), [])
        own_sums[1] = after(own_sums[1], mine)
        line.add_near(line.far_in, mine)
    else:
        attended = attend(ids, queries, blocks, 0)
        partial = jnp.concatenate(
            [mixed_term(jnp.int32(s), []) for s in range(count)], axis=1
        )
        mixed = lax.psum_scatter(partial, "tensor", scatter_dimension=1, tiled=True)
        grads = None
        for at in range(count):
            last = at == count - 1
            grads = back_project(
                groups[at : at + 1], w_out, grads, jnp.bfloat16 if last else jnp.float32
            )
        own_sums = [grad_part(ids, part) for part in range(parts)]
    returned = [
        lax.all_to_all(part, "dp", split_axis=0, concat_axis=0, tiled=True) for part in own_sums
    ]
    d_kv = settle(serving_slot, returned)
    if by_line:
        mine = sum_of([after(mine, d_kv), line.beside_in, line.far_in])
        mixed = sum_of([mine, line.near_in])
    return (mixed, d_kv)


def solution(mesh):
    placed = (
        P("tensor", "dp", None),
        P("dp", "tensor"),
        P("tensor", None),
        P("dp", "tensor"),
        P(),
        P(),
    )
    return jax.shard_map(
        local,
        mesh=mesh,
        in_specs=placed,
        out_specs=(P("dp", "tensor"), P("dp", "tensor")),
        check_vma=False,
    )
```
